32 devices in a mesh: patch: 8 (over z, y), trial: 4 (over x, core).
Axes of the slice: x: 2, y: 2, z: 4, core: 2. Of those that a mesh axis runs over, the one named last changes fastest.
Arguments:
- activity: float32 [32, 32768], P('trial', 'patch'), may hold values from 0 to 1
- history: bfloat16 [7, 32, 32768], P(None, 'trial', 'patch'), may hold values from 0 to 1
- drive: float32 [32768], P('patch'), may hold values from -6 to 6
- slope: float32 [32], P('trial'), may hold values from 0.5 to 2
- strength: float32 [32], P('trial'), may hold values from 0.1 to 1
- kernel: bfloat16 [256, 4, 128, 128], P('patch', 'trial'), may hold values from -0.25 to 0.25
- kernel_index: int32 [256, 4], P('patch'), may hold values from 0 to 33, as said below
- tract_source: int32 [1024], P('patch'), may hold values from 0 to 31
- tract_delay: int32 [1024], P('patch'), may hold values from 4 to 7
- tract_target: int32 [1024, 1], P('patch'), may hold values from 0 to 7; in each aligned block of 128 rows (0 to 127, 128 to 255, ...) at most 17 rows name the same one
- tract_block: int32 [1024], P('patch'), may hold values from 0 to 31
- tract_weight: float32 [1024], P('patch'), may hold values from 0.25 to 2
- voxel_owner: int32 [32768], P('patch'), may hold values from 0 to 991, as said below
- vaso_signal: float32 [32, 1024], P('trial', 'patch'), may hold values from -3 to 3
- blood_flow: float32 [32, 1024], P('trial', 'patch'), may hold values from 0.5 to 1.5
Outputs:
- activity_out: float32 [32, 32768], P('trial', 'patch')
- vaso_out: float32 [32, 1024], P('trial', 'patch')
- flow_out: float32 [32, 1024], P('trial', 'patch')
The draws below stay inside these ranges and needn't reach their ends.
Inputs may be any that keep to these rules, and one draw needn't show every extreme that they name: `kernel_index`: block b of a patch lists itself (entry b + 1) first; its other entries name b, b + 1 or b + 2; block 0's second entry is 0 and the last block's third entry is 33. `tract_target`: among the 128 tracts of one patch no target patch is named more than 17 times. `voxel_owner`: A vertex of patch p lies in a voxel owned by patch p - 1, p or p + 1, where patch p owns voxels p * 128 to (p + 1) * 128 - 1; the last quarter of each patch's voxels hold no vertex.
All inputs are finite; a program needn't handle non-finite values.
Results may differ from the reference program's by a relative error of at most 0.00037.
Values may be sent and summed in bfloat16 or wider, within the bound.
A program may use at most 64 MiB of HBM per device.

```python
import math
import jax
import jax.numpy as jnp
import numpy as np
from jax import lax

VP = 4096
BLOCK = 128
NEAR = 4
STEPS = 4
TRB = 128
VOXD = 128
HIST = 7
NBLK = 32
NB = 256
NV = 32768
TRIALS = 32
TRACTS = 1024
CAP = 17
NVOX = 1024
N_PATCH = 8


def draw_kernel_index(key, part):
    nblk = VP // BLOCK
    nblocks = nblk * N_PATCH
    own = jnp.arange(nblocks, dtype=jnp.int32) % nblk
    extra = jax.random.randint(key, (nblocks, NEAR - 1), 0, 3).astype(jnp.int32)
    others = own[:, None] + extra
    others = others.at[:, 0].set(jnp.where(own == 0, 0, others[:, 0]))
    others = others.at[:, 1].set(jnp.where(own == nblk - 1, nblk + 1, others[:, 1]))
    return jnp.concatenate([(own + 1)[:, None], others], axis=1).astype(jnp.int32)


def draw_voxel_owner(key, part):
    count = VP * N_PATCH
    first = jax.random.fold_in(key, 11)
    second = jax.random.fold_in(key, 23)
    home = jnp.arange(count, dtype=jnp.int32) // VP
    pick = jax.random.randint(first, (count,), 0, 8)
    moved = jnp.where(pick == 0, -1, jnp.where(pick == 1, 1, 0)).astype(jnp.int32)
    owner = jnp.clip(home + moved, 0, N_PATCH - 1)
    inner = jax.random.randint(second, (count,), 0, VOXD * 3 // 4).astype(jnp.int32)
    return (owner * VOXD + inner).astype(jnp.int32)


def plant(drawn, stream_key, low, largest):
    dims = drawn.shape
    index_at = [jax.random.randint(jax.random.fold_in(stream_key, axis), (), 0, dims[axis]) for axis in range(len(dims))]
    drawn = drawn.at[tuple(index_at)].set(low)
    longest = dims.index(max(dims))
    index_at[longest] = (index_at[longest] + 1) % dims[longest]
    return drawn.at[tuple(index_at)].set(largest)


def steps_of(own_key, dims, pieces, low, top_value):
    loudness, own = 1.0, jax.random.fold_in(own_key, 6)
    for position, shards_of in pieces:
        draws = jnp.exp(jax.random.uniform(jax.random.fold_in(own, position), (shards_of,), jnp.float32, low / len(pieces), top_value / len(pieces)))
        loudness = loudness * jnp.repeat(draws, dims[position] // shards_of).reshape([-1 if axis == position else 1 for axis in range(len(dims))])
    return loudness


def assign_block(own_key, own, number, rows, number_of, top, bound, skew):
    sequence = jax.random.permutation(own_key, number_of)
    packed, usual = load_shares(number_of, rows * top, bound, skew, True), load_shares(number_of, rows * top, bound, skew, False)
    places = jnp.arange(number_of)

    def named(tallies, turn):
        used = int((tallies > 0).sum())
        fixed = max(1, used // 4)
        passed = fixed + (places - fixed + turn * (used - fixed)) % max(1, number_of - fixed)
        return jnp.zeros((number_of,), jnp.int32).at[sequence[jnp.where(places < fixed, places, passed)]].set(jnp.asarray(tallies, jnp.int32))

    tallies = jnp.where(number % 4 == 0, named(packed, number // 4), named(usual, number - number // 4 - 1))
    mixed = jax.random.permutation(jax.random.fold_in(own, 3), number_of)
    donor, sink = mixed[0:number_of // 2 * 2:2], mixed[1:number_of // 2 * 2:2]
    margin = jnp.minimum(tallies[donor] - 1, bound - tallies[sink]) // 2
    margin = jnp.where((donor == sequence[0]) | (sink == sequence[0]) | (tallies[sink] == 0), 0, jnp.maximum(margin, 0))
    passed = jax.random.randint(jax.random.fold_in(own, 4), (number_of // 2,), 0, 1 << 20) % (margin + 1)
    tallies = tallies.at[donor].add(-passed).at[sink].add(passed)
    items = jnp.searchsorted(jnp.cumsum(tallies), jnp.arange(rows * top), side="right").astype(jnp.int32)
    listing = items.reshape(top, rows).T
    listing = listing[jax.random.permutation(jax.random.fold_in(own, 1), rows)]
    turn = jax.random.randint(jax.random.fold_in(own, 2), (rows, 1), 0, top)
    return jnp.take_along_axis(listing, (jnp.arange(top)[None, :] + turn) % top, axis=1)


def load_shares(amount, total, bound, skew, full):
    weights = [(1 << 20) // math.isqrt(standing ** skew) + 1 for standing in range(1, amount + 1)]
    largest = bound if full else min(bound, max(-(-total // amount), total * weights[0] // sum(weights)))
    least = 1 if total - largest >= amount - 1 else 0
    given, surplus = [largest] + [least] * (amount - 1), total - largest - least * (amount - 1)
    while surplus > 0:
        candidates = [i for i in range(1, amount) if given[i] < largest] or [i for i in range(1, amount) if given[i] < bound]
        pool, remaining = sum([weights[i] for i in candidates]), surplus
        for i in candidates:
            more = min(bound - given[i], max(1, remaining * weights[i] // pool), surplus)
            given[i] = given[i] + more
            surplus = surplus - more
    return np.array(given)


def centred(key, dims, scale, most, cuts=(), held_as=jnp.bfloat16):
    factor_of = steps_of(key, dims, cuts, -0.22, 0.18) if cuts else 1.0
    result = jax.random.normal(key, dims, jnp.float32) * scale * factor_of
    return jnp.minimum(jnp.maximum(result, -most), most).astype(held_as)


def setup_inputs(seed: int = 0) -> dict:
    key_of = jax.random.split(jax.random.key(seed), 16)
    activity = jnp.clip(1.0 * jax.random.uniform(key_of[0], (TRIALS, NV), jnp.float32) ** steps_of(key_of[0], (TRIALS, NV), ((0, 4), (1, 8)), -0.2, 0.2), 0.0, 1.0)
    history = jnp.clip(1.0 * jax.random.uniform(key_of[1], (HIST, TRIALS, NV), jnp.float32) ** steps_of(key_of[1], (HIST, TRIALS, NV), ((1, 4), (2, 8)), -0.2, 0.2), 0.0, 1.0).astype(jnp.bfloat16)
    drive = centred(key_of[2], (NV,), 1.0, 6.0, ((0, 8),), jnp.float32)
    slope = jnp.clip(jnp.exp(math.log(2.0) - 1.3862944 * jax.random.uniform(key_of[3], (TRIALS,), jnp.float32) ** steps_of(key_of[3], (TRIALS,), ((0, 4),), -0.2, 0.2)), 0.5, 2.0)
    strength = jnp.clip(jnp.exp(math.log(1.0) - 2.3025851 * jax.random.uniform(key_of[4], (TRIALS,), jnp.float32) ** steps_of(key_of[4], (TRIALS,), ((0, 4),), -0.2, 0.2)), 0.1, 1.0)
    kernel = centred(key_of[5], (NB, NEAR, BLOCK, BLOCK), (NEAR * BLOCK) ** -0.5, 0.25, ((0, 8), (1, 4)))
    kernel_index = draw_kernel_index(jax.random.fold_in(key_of[15], 71), 0)
    tract_source = plant(jax.random.randint(key_of[7], (TRACTS,), 0, NBLK), jax.random.fold_in(key_of[7], 1), 0, NBLK - 1).astype(jnp.int32)
    tract_delay = plant(jax.random.randint(key_of[8], (TRACTS,), STEPS, 2 * STEPS), jax.random.fold_in(key_of[8], 1), STEPS, (2 * STEPS) - 1).astype(jnp.int32)
    tract_target_keys = jax.random.split(jax.random.fold_in(key_of[9], 1), TRACTS // TRB)
    tract_target_turns = jax.random.permutation(jax.random.fold_in(key_of[9], 3), TRACTS // TRB)
    tract_target = jax.vmap(lambda own, number: assign_block(jax.random.fold_in(key_of[9], 2), own, number, TRB, N_PATCH, 1, CAP, 1))(tract_target_keys, tract_target_turns).reshape((TRACTS, 1))
    tract_block = plant(jax.random.randint(key_of[10], (TRACTS,), 0, NBLK), jax.random.fold_in(key_of[10], 1), 0, NBLK - 1).astype(jnp.int32)
    tract_weight = jnp.clip(jnp.exp(math.log(2.0) - 2.0794415 * jax.random.uniform(key_of[11], (TRACTS,), jnp.float32) ** steps_of(key_of[11], (TRACTS,), ((0, 8),), -0.2, 0.2)), 0.25, 2.0)
    voxel_owner = draw_voxel_owner(jax.random.fold_in(key_of[15], 71), 0)
    vaso_signal = centred(key_of[13], (TRIALS, NVOX), 0.5, 3.0, ((0, 4), (1, 8)), jnp.float32)
    blood_flow = jnp.clip(1.0 + 0.1 * jax.random.normal(key_of[14], (TRIALS, NVOX), jnp.float32), 0.5, 1.5)
    return {"activity": activity, "history": history, "drive": drive, "slope": slope, "strength": strength, "kernel": kernel, "kernel_index": kernel_index, "tract_source": tract_source, "tract_delay": tract_delay, "tract_target": tract_target, "tract_block": tract_block, "tract_weight": tract_weight, "voxel_owner": voxel_owner, "vaso_signal": vaso_signal, "blood_flow": blood_flow}


def reference(activity, history, drive, slope, strength, kernel, kernel_index, tract_source, tract_delay, tract_target, tract_block, tract_weight, voxel_owner, vaso_signal, blood_flow):
    nblk = VP // BLOCK
    nblocks = nblk * N_PATCH
    kidx = kernel_index.reshape(N_PATCH, nblk, NEAR)
    kern = kernel.reshape(N_PATCH, nblk, NEAR, BLOCK, BLOCK)
    source = (jnp.arange(TRB * N_PATCH, dtype=jnp.int32) // TRB) * nblk + tract_source
    target = tract_target[:, 0] * nblk + tract_block
    hist_blocks = history.reshape(HIST, TRIALS, nblocks, BLOCK)
    coupling = []
    for step in range(STEPS):
        lag = (tract_delay - step - 1).astype(jnp.int32)
        rows = hist_blocks[lag, :, source, :]
        sent = (rows.astype(jnp.float32) * tract_weight[:, None, None]).astype(jnp.bfloat16)
        summed = jax.ops.segment_sum(sent.astype(jnp.float32), target, nblocks)
        coupling.append(summed.transpose(1, 0, 2).reshape(TRIALS, VP * N_PATCH))

    def one_patch(args):
        extended, index, tiles = args
        picked = extended[:, index]
        return jnp.einsum("tbki,bkij->tbj", picked.astype(jnp.float32), tiles.astype(jnp.float32))

    counts = jax.ops.segment_sum(jnp.ones((VP * N_PATCH,), jnp.float32), voxel_owner, VOXD * N_PATCH)
    floor = jnp.maximum(counts, 1.0)
    rate = activity
    vaso = vaso_signal
    flow = blood_flow
    for step in range(STEPS):
        rate_b = rate.astype(jnp.bfloat16).reshape(TRIALS, N_PATCH, VP)
        zero = jnp.zeros((TRIALS, 1, BLOCK), jnp.bfloat16)
        left = jnp.concatenate([zero, rate_b[:, :-1, VP - BLOCK:]], axis=1)
        right = jnp.concatenate([rate_b[:, 1:, :BLOCK], zero], axis=1)
        extended = jnp.concatenate([left, rate_b, right], axis=2).reshape(TRIALS, N_PATCH, nblk + 2, BLOCK)
        local = lax.map(one_patch, (extended.transpose(1, 0, 2, 3), kidx, kern))
        local = local.transpose(1, 0, 2, 3).reshape(TRIALS, VP * N_PATCH)
        pre = slope[:, None] * (local + strength[:, None] * coupling[step] + drive[None, :])
        rate = rate + 0.5 * (jax.nn.sigmoid(pre) - rate)
        level = jax.ops.segment_sum(rate.T, voxel_owner, VOXD * N_PATCH).T / floor[None, :]
        vaso = vaso + 0.5 * (level - 0.65 * vaso - 0.41 * (flow - 1.0))
        flow = flow + 0.5 * vaso
    return rate, vaso, flow
```

```python
import functools

import jax
import jax.numpy as jnp
from jax import lax
from jax.experimental import pallas as pl
from jax.experimental.pallas import tpu as pltpu
from jax.sharding import PartitionSpec as P

BLOCK = 128
STEPS = 4
HIST = 7
CHUNKS = 4
MESH = pl.DeviceIdType.MESH


def extended_2(array, sides, width):
    for axis, dim in sides:
        peers, length = (lax.axis_size(axis), array.shape[dim])
        up = [(i, (i + 1) % peers) for i in range(peers - 1)]
        down = [(j, i) for i, j in up]
        last = lax.slice_in_dim(array, length - width, length, axis=dim)
        leading = lax.slice_in_dim(array, 0, width, axis=dim)
        before = lax.ppermute(last, axis, up)
        after = lax.ppermute(leading, axis, down)
        array = jnp.concatenate([before, array, after], axis=dim)
    return array


def shards(
    activity,
    history,
    drive,
    slope,
    strength,
    kernel,
    kernel_index,
    tract_source,
    tract_delay,
    tract_target,
    tract_block,
    tract_weight,
    voxel_owner,
    vaso_signal,
    blood_flow,
):
    trials_here = activity.shape[0]
    verts = activity.shape[1]
    nblk = verts // BLOCK
    patches = lax.axis_size("patch")
    tracts_here = tract_source.shape[0]
    capacity = max(2, tracts_here // patches + 1)
    slots = patches * capacity
    voxels_here = vaso_signal.shape[1]
    hist_blocks = history.reshape(HIST, trials_here, nblk, BLOCK)
    lag = tract_delay[:, None] - jnp.arange(STEPS, dtype=jnp.int32)[None, :] - 1
    rows = hist_blocks[lag, :, tract_source[:, None], :]
    weighted = (rows.astype(jnp.float32) * tract_weight[:, None, None, None]).astype(jnp.bfloat16)
    target = tract_target[:, 0]
    order = jnp.arange(tracts_here, dtype=jnp.int32)
    same = (target[:, None] == target[None, :]) & (order[None, :] < order[:, None])
    rank = jnp.sum(same.astype(jnp.int32), axis=1)
    slot = target * capacity + rank
    send_rates = jnp.zeros((slots, STEPS, trials_here, BLOCK), jnp.bfloat16).at[slot].set(weighted)
    send_blocks = jnp.full((slots,), -1, jnp.int32).at[slot].set(tract_block)
    got_rates, got_blocks = (
        lax.all_to_all(send_rates, "patch", split_axis=0, concat_axis=0, tiled=True),
        lax.all_to_all(send_blocks, "patch", split_axis=0, concat_axis=0, tiled=True),
    )
    onehot = (got_blocks[None, :] == jnp.arange(nblk, dtype=jnp.int32)[:, None]).astype(
        jnp.bfloat16
    )
    coupling = jnp.einsum("bs,sxtj->xtbj", onehot, got_rates, preferred_element_type=jnp.float32)
    coupling = coupling.reshape(STEPS, trials_here, verts)
    tiles = lax.all_gather(kernel, "trial", axis=1, tiled=True)
    rate = activity
    recorded = []
    for step in range(STEPS):
        rate_b = rate.astype(jnp.bfloat16)
        extended = extended_2(rate_b, (("patch", 1),), BLOCK)
        extended = extended.reshape(trials_here, nblk + 2, BLOCK)
        picked = extended[:, kernel_index]
        local = jnp.einsum("tbki,bkij->tbj", picked, tiles, preferred_element_type=jnp.float32)
        local = local.reshape(trials_here, verts)
        pre = slope[:, None] * (local + strength[:, None] * coupling[step] + drive[None, :])
        rate = rate + 0.5 * (jax.nn.sigmoid(pre) - rate)
        recorded.append(rate)
    values = jnp.concatenate(
        [
            jnp.stack(recorded).reshape(STEPS * trials_here, verts),
            jnp.ones((1, verts), jnp.float32),
        ],
        axis=0,
    )
    offset = (lax.axis_index("patch") - 1) * voxels_here
    partial_value = (
        jnp.zeros((values.shape[0], 3 * voxels_here), jnp.float32)
        .at[:, voxel_owner - offset]
        .add(values)
    )
    widened = extended_2(partial_value, (("patch", 1),), voxels_here)
    mine = (
        widened[:, :voxels_here]
        + widened[:, 2 * voxels_here : 3 * voxels_here]
        + widened[:, 4 * voxels_here :]
    )
    floor = jnp.maximum(mine[-1], 1.0)
    levels = mine[:-1].reshape(STEPS, trials_here, voxels_here) / floor[None, None, :]
    vaso = vaso_signal
    flow = blood_flow
    for step in range(STEPS):
        vaso = vaso + 0.5 * (levels[step] - 0.65 * vaso - 0.41 * (flow - 1.0))
        flow = flow + 0.5 * vaso
    return (rate, vaso, flow)


def window(
    patches,
    groups,
    act_ref,
    hist_ref,
    drive_ref,
    slope_ref,
    strength_ref,
    kern_ref,
    index_ref,
    source_ref,
    delay_ref,
    target_ref,
    block_ref,
    weight_ref,
    owner_ref,
    vaso_ref,
    flow_ref,
    act_out,
    vaso_out,
    flow_out,
    ht,
    hist2,
    send,
    recv,
    over_f,
    over_send,
    over_recv,
    meta_send,
    meta_recv,
    tiles,
    ext,
    halo_send,
    halo,
    coupling,
    owned,
    vox_send,
    vox,
    send_sem,
    recv_sem,
    osend_sem,
    orecv_sem,
    msend_sem,
    mrecv_sem,
    xsend_sem,
    xrecv_sem,
    rsend_sem,
    rrecv_sem,
    csem,
    hsend_sem,
    hrecv_sem,
    vsend_sem,
    vrecv_sem,
    local_sem,
):
    f32, bf16, i32 = jnp.float32, jnp.bfloat16, jnp.int32
    n = patches
    nblk = 32
    me = lax.axis_index("patch")
    grp = lax.axis_index("trial")
    far = lax.rem(grp + 2, groups)
    near = grp + 1 - 2 * lax.rem(grp, 2)

    barrier = pltpu.get_barrier_semaphore()
    for d in range(1, n):
        pl.semaphore_signal(
            barrier, inc=1, device_id={"patch": lax.rem(me + d, n)}, device_id_type=MESH
        )
    for g in (far, near):
        pl.semaphore_signal(barrier, inc=1, device_id={"trial": g}, device_id_type=MESH)

    def remote(src, dst, ssem, rsem, where):
        return pltpu.make_async_remote_copy(
            src_ref=src,
            dst_ref=dst,
            send_sem=ssem,
            recv_sem=rsem,
            device_id=where,
            device_id_type=MESH,
        )

    def part(c):
        return pl.ds(c * (nblk // CHUNKS), nblk // CHUNKS)

    own_tiles = pltpu.make_async_copy(kern_ref, tiles.at[grp], local_sem)
    own_tiles.start()

    def tile_far(k, c):
        return remote(
            kern_ref.at[part(c)],
            tiles.at[k, part(c)],
            xsend_sem.at[c],
            xrecv_sem.at[c],
            {"trial": far},
        )

    def tile_near(k):
        return remote(kern_ref, tiles.at[k], csem.at[0], csem.at[1], {"trial": near})

    def tile_relay(k, c):
        return remote(
            tiles.at[k, part(c)],
            tiles.at[k, part(c)],
            rsend_sem.at[c],
            rrecv_sem.at[c],
            {"trial": near},
        )

    def main_copy(s, p, q):
        return remote(
            send.at[s, pl.ds(pl.multiple_of(q * 16, 16), 16)],
            recv.at[s, pl.ds(pl.multiple_of(p * 16, 16), 16)],
            send_sem.at[s, q],
            recv_sem.at[s, p],
            {"patch": q},
        )

    def over_copy(p, q):
        return remote(
            over_send.at[q], over_recv.at[p], osend_sem.at[q], orecv_sem.at[p], {"patch": q}
        )

    def meta_copy(p, q):
        return remote(
            meta_send.at[q], meta_recv.at[p], msend_sem.at[q], mrecv_sem.at[p], {"patch": q}
        )

    def halo_copy(s, side):
        where = me + 1 if side == 0 else me - 1
        return remote(
            halo_send.at[s, side],
            halo.at[s, side],
            hsend_sem.at[s, side],
            hrecv_sem.at[s, side],
            {"patch": where},
        )

    def vox_copy(side):
        where = me + 1 if side == 0 else me - 1
        return remote(
            vox_send.at[side], vox.at[side], vsend_sem.at[side], vrecv_sem.at[side], {"patch": where}
        )

    has_left, has_right = me > 0, me < n - 1

    def halo_start(s):
        halo_send[s, 0] = ext[s, nblk]
        halo_send[s, 1] = ext[s, 1]

        @pl.when(has_right)
        def _():
            halo_copy(s, 0).start()

        @pl.when(has_left)
        def _():
            halo_copy(s, 1).start()

    def halo_take(s):
        @pl.when(has_left)
        def _():
            halo_copy(s, 0).wait_recv()
            ext[s, 0] = halo[s, 0]

        @pl.when(has_right)
        def _():
            halo_copy(s, 1).wait_recv()
            ext[s, nblk + 1] = halo[s, 1]

    sub = lax.broadcasted_iota(i32, (128, 128), 0)
    lane = lax.broadcasted_iota(i32, (128, 128), 1)
    eye = sub == lane

    def row_of(col):
        return jnp.sum(jnp.where(eye, col, 0.0), axis=0, keepdims=True)

    target_col = jnp.broadcast_to(target_ref[...].astype(f32), (128, 128))
    target_row = row_of(target_col)
    same = target_col == target_row
    rank_row = jnp.sum(jnp.where(same & (sub < lane), 1.0, 0.0), axis=0, keepdims=True)
    rank_col = jnp.sum(jnp.where(same & (lane < sub), 1.0, 0.0), axis=1, keepdims=True)
    key_row = ((delay_ref[...] - 1) * nblk + source_ref[...]).astype(f32)
    weight_row = weight_ref[...]
    slot_row = jnp.where(rank_row < 16.0, target_row * 16.0 + rank_row, -1.0)
    sel = sub.astype(f32) == slot_row
    q8 = lax.broadcasted_iota(i32, (n, 128), 0).astype(f32)
    sel_over = (q8 == target_row) & (rank_row == 16.0)

    def pick(mask, row):
        return jnp.sum(jnp.where(mask, row, 0.0), axis=1, keepdims=True)

    key = pick(sel, key_row)
    weight = pick(sel, weight_row)
    key_over = pick(sel_over, key_row)
    weight_over = pick(sel_over, weight_row)

    def turn(lag, _):
        old = hist_ref[lag].astype(f32)
        for b in range(nblk):
            ht[lag, pl.ds(b, 8, stride=nblk), :] = old[:, b * 128 : (b + 1) * 128]
        rows = pl.ds(pl.multiple_of(lag * nblk, nblk), nblk)
        for j in range(8):
            hist2[rows, j * 128 : (j + 1) * 128] = ht[lag, j * nblk : (j + 1) * nblk, :].astype(bf16)
        return 0

    lax.fori_loop(0, HIST, turn, 0)
    hist2[HIST * nblk :, :] = jnp.zeros((nblk, 1024), bf16)

    wide = lax.broadcasted_iota(i32, (128, 256), 1).astype(f32)
    wide8 = lax.broadcasted_iota(i32, (n, 256), 1).astype(f32)

    def gathered(s):
        choose = jnp.where(wide == key - float(s * nblk), 1.0, 0.0).astype(bf16)
        rows = jnp.dot(choose, hist2[...], preferred_element_type=f32)
        send[s] = (rows * weight).astype(bf16)

    gathered(0)

    a = jnp.where(q8 == target_row, block_ref[...].astype(f32), 0.0).astype(bf16)
    lanes = lane.astype(f32)
    mef = me.astype(f32)
    b1 = jnp.where((rank_col < 16.0) & (lanes == rank_col + mef * 16.0), 1.0, 0.0).astype(bf16)
    b2 = jnp.where((rank_col == 16.0) & (lanes == mef), 1.0, 0.0).astype(bf16)
    m1 = jnp.dot(a, b1, preferred_element_type=f32)
    m2 = jnp.dot(a, b2, preferred_element_type=f32)
    m = jnp.concatenate([m1, m2], axis=1)
    for q in range(n):
        meta_send[q] = jnp.broadcast_to(m[q : q + 1], (8, 256))

    for b in range(nblk):
        ext[0, b + 1] = act_ref[:, b * 128 : (b + 1) * 128]
    for s in range(STEPS):
        ext[s, 0] = jnp.zeros((8, 128), f32)
        ext[s, nblk + 1] = jnp.zeros((8, 128), f32)

    pl.semaphore_wait(barrier, n + 1)
    for c in range(CHUNKS):
        tile_far(grp, c).start()
    for d in range(1, n):
        main_copy(0, me, lax.rem(me + d, n)).start()
    tile_near(grp).start()
    halo_start(0)
    for d in range(1, n):
        meta_copy(me, lax.rem(me + d, n)).start()
    for s in range(1, STEPS):
        gathered(s)
        for d in range(1, n):
            main_copy(s, me, lax.rem(me + d, n)).start()
        if s == 1:
            choose = jnp.concatenate(
                [jnp.where(wide8 == key_over - float(t * nblk), 1.0, 0.0) for t in range(STEPS)],
                axis=0,
            ).astype(bf16)
            rows = jnp.dot(choose, hist2[...], preferred_element_type=f32)
            for t in range(STEPS):
                for j in range(8):
                    over_f[pl.ds(t * 8 + j, n, stride=32), :] = (
                        rows[t * 8 : t * 8 + 8, j * 128 : (j + 1) * 128] * weight_over
                    )
            for q in range(n):
                over_send[q] = over_f[q * 32 : (q + 1) * 32, :].astype(bf16)
            for d in range(1, n):
                over_copy(me, lax.rem(me + d, n)).start()

    mine16 = pl.ds(pl.multiple_of(me * 16, 16), 16)
    for s in range(STEPS):
        recv[s, mine16, :] = send[s, mine16, :]
    over_recv[me] = over_send[me]
    meta_recv[me] = meta_send[me]

    first = ((me - 1) * 128).astype(f32)
    vox_id = lax.broadcasted_iota(i32, (384, 128), 0).astype(f32) + first

    def member(b, _):
        owner = owner_ref[pl.ds(b, 1), :].astype(f32)
        owned[b] = jnp.where(vox_id == owner, 1.0, 0.0).astype(bf16)
        return 0

    lax.fori_loop(0, nblk, member, 0)

    eye8 = lax.broadcasted_iota(i32, (8, 8), 0) == lax.broadcasted_iota(i32, (8, 8), 1)
    slope = jnp.sum(jnp.where(eye8, slope_ref[...], 0.0), axis=1, keepdims=True)
    strength = jnp.sum(jnp.where(eye8, strength_ref[...], 0.0), axis=1, keepdims=True)
    slope = jnp.broadcast_to(slope, (8, 128))
    strength = jnp.broadcast_to(strength, (8, 128))

    for d in range(1, n):
        p = lax.rem(me + d, n)
        meta_copy(p, me).wait_recv()
        over_copy(p, me).wait_recv()
    where_row = meta_recv[0]
    for p in range(1, n):
        where_row = where_row + meta_recv[p]
    where_row = where_row[0:1, 0:144]
    onehot = jnp.where(
        lax.broadcasted_iota(i32, (nblk, 144), 0).astype(f32) == where_row, 1.0, 0.0
    ).astype(bf16)
    for p in range(n):
        over_f[p * 32 : (p + 1) * 32, :] = over_recv[p].astype(f32)
    for s in range(STEPS):
        extra = jnp.concatenate(
            [over_f[pl.ds(s * 8 + j, n, stride=32), :] for j in range(8)], axis=1
        )
        recv[s, 128:144, :] = jnp.concatenate([extra, jnp.zeros_like(extra)], axis=0).astype(bf16)

    def couple(s):
        for d in range(1, n):
            main_copy(s, lax.rem(me + d, n), me).wait_recv()
        total = jnp.dot(onehot, recv[s], preferred_element_type=f32)
        for j in range(8):
            coupling[s, j * nblk : (j + 1) * nblk, :] = total[:, j * 128 : (j + 1) * 128]

    def update(s, b):
        lhs = jnp.concatenate([ext[s, index_ref[b, k]] for k in range(4)], axis=1).astype(bf16)
        rhs = jnp.concatenate([tiles[k, b] for k in range(4)], axis=0)
        local = jnp.dot(lhs, rhs, preferred_element_type=f32)
        tract = coupling[s, pl.ds(b, 8, stride=nblk), :]
        pre = slope * (local + strength * tract + drive_ref[pl.ds(b, 1), :])
        rate = ext[s, b + 1]
        ext[s + 1, b + 1] = rate + 0.5 * (jax.nn.sigmoid(pre) - rate)

    def updates(s, low, high, width):
        def some(i, _):
            for u in range(width):
                update(s, low + i * width + u)
            return 0

        lax.fori_loop(0, (high - low) // width, some, 0)

    couple(0)
    halo_take(0)
    own_tiles.wait()
    tile_near(near).wait_recv()
    tile_far(far, 0).wait_recv()
    tile_relay(far, 0).start()
    other = lax.rem(near + 2, groups)
    for c in range(CHUNKS):
        if c + 1 < CHUNKS:
            tile_far(far, c + 1).wait_recv()
            tile_relay(far, c + 1).start()
        tile_relay(other, c).wait_recv()
        updates(0, c * (nblk // CHUNKS), (c + 1) * (nblk // CHUNKS), nblk // CHUNKS)
    halo_start(1)

    for s in range(1, STEPS):
        couple(s)
        updates(s, 1, nblk - 1, 10)
        halo_take(s)
        update(s, 0)
        update(s, nblk - 1)
        if s + 1 < STEPS:
            halo_start(s + 1)

    ones = jnp.ones((16, 512), bf16)

    def sums(i, total):
        rates = [
            jnp.concatenate([ext[s + 1, i * 4 + u + 1] for u in range(4)], axis=1)
            for s in range(STEPS)
        ]
        rates = jnp.concatenate(rates, axis=0)
        high = rates.astype(bf16)
        low = (rates - high.astype(f32)).astype(bf16)
        lhs = jnp.concatenate([high, low, ones], axis=0)
        rhs = jnp.concatenate([owned[i * 4 + u] for u in range(4)], axis=1)
        return total + lax.dot_general(
            lhs, rhs, (((1,), (1,)), ((), ())), preferred_element_type=f32
        )

    total = lax.fori_loop(0, nblk // 4, sums, jnp.zeros((80, 384), f32))
    total = jnp.concatenate([total[0:32] + total[32:64], total[64:72]], axis=0)
    vox_send[0] = total[:, 256:384]
    vox_send[1] = total[:, 0:128]

    @pl.when(has_right)
    def _():
        vox_copy(0).start()

    @pl.when(has_left)
    def _():
        vox_copy(1).start()

    vox_send[2] = total[:, 128:256]
    for b in range(nblk):
        act_out[:, b * 128 : (b + 1) * 128] = ext[STEPS, b + 1]

    @pl.when(has_left)
    def _():
        vox_copy(0).wait_recv()
        vox_send[2] = vox_send[2] + vox[0]

    @pl.when(has_right)
    def _():
        vox_copy(1).wait_recv()
        vox_send[2] = vox_send[2] + vox[1]

    floor = jnp.maximum(vox_send[2, 32:40, :], 1.0)
    vaso = vaso_ref[...]
    flow = flow_ref[...]
    for s in range(STEPS):
        level = vox_send[2, s * 8 : s * 8 + 8, :] / floor
        vaso = vaso + 0.5 * (level - 0.65 * vaso - 0.41 * (flow - 1.0))
        flow = flow + 0.5 * vaso
    vaso_out[...] = vaso
    flow_out[...] = flow

    for d in range(1, n):
        q = lax.rem(me + d, n)
        for s in range(STEPS):
            main_copy(s, me, q).wait_send()
        over_copy(me, q).wait_send()
        meta_copy(me, q).wait_send()
    tile_near(grp).wait_send()
    for c in range(CHUNKS):
        tile_far(grp, c).wait_send()
        tile_relay(far, c).wait_send()

    @pl.when(has_right)
    def _():
        for s in range(STEPS):
            halo_copy(s, 0).wait_send()
        vox_copy(0).wait_send()

    @pl.when(has_left)
    def _():
        for s in range(STEPS):
            halo_copy(s, 1).wait_send()
        vox_copy(1).wait_send()


def fused(
    activity,
    history,
    drive,
    slope,
    strength,
    kernel,
    kernel_index,
    tract_source,
    tract_delay,
    tract_target,
    tract_block,
    tract_weight,
    voxel_owner,
    vaso_signal,
    blood_flow,
):
    n, groups = lax.axis_size("patch"), lax.axis_size("trial")
    f32, bf16 = jnp.float32, jnp.bfloat16
    vmem = pl.BlockSpec(memory_space=pltpu.VMEM)
    smem = pl.BlockSpec(memory_space=pltpu.SMEM)
    dma = pltpu.SemaphoreType.DMA
    scratch = [
        pltpu.VMEM((HIST, 256, 128), f32),
        pltpu.VMEM((256, 1024), bf16),
        pltpu.VMEM((STEPS, 128, 1024), bf16),
        pltpu.VMEM((STEPS, 144, 1024), bf16),
        pltpu.VMEM((256, 128), f32),
        pltpu.VMEM((n, 32, 128), bf16),
        pltpu.VMEM((n, 32, 128), bf16),
        pltpu.VMEM((n, 8, 256), f32),
        pltpu.VMEM((n, 8, 256), f32),
        pltpu.VMEM((4, 32, 128, 128), bf16),
        pltpu.VMEM((STEPS + 1, 34, 8, 128), f32),
        pltpu.VMEM((STEPS, 2, 8, 128), f32),
        pltpu.VMEM((STEPS, 2, 8, 128), f32),
        pltpu.VMEM((STEPS, 256, 128), f32),
        pltpu.VMEM((32, 384, 128), bf16),
        pltpu.VMEM((3, 40, 128), f32),
        pltpu.VMEM((2, 40, 128), f32),
        dma((STEPS, n)),
        dma((STEPS, n)),
        dma((n,)),
        dma((n,)),
        dma((n,)),
        dma((n,)),
        dma((CHUNKS,)),
        dma((CHUNKS,)),
        dma((CHUNKS,)),
        dma((CHUNKS,)),
        dma((2,)),
        dma((STEPS, 2)),
        dma((STEPS, 2)),
        dma((2,)),
        dma((2,)),
        dma,
    ]
    return pl.pallas_call(
        functools.partial(window, n, groups),
        out_shape=(
            jax.ShapeDtypeStruct(activity.shape, f32),
            jax.ShapeDtypeStruct(vaso_signal.shape, f32),
            jax.ShapeDtypeStruct(blood_flow.shape, f32),
        ),
        in_specs=[vmem] * 6 + [smem] + [vmem] * 8,
        out_specs=(vmem, vmem, vmem),
        scratch_shapes=scratch,
        compiler_params=pltpu.CompilerParams(
            collective_id=0, has_side_effects=True, vmem_limit_bytes=40 * 1024 * 1024
        ),
    )(
        activity,
        history,
        drive.reshape(32, 128),
        slope.reshape(1, 8),
        strength.reshape(1, 8),
        kernel.reshape(32, 128, 128),
        kernel_index,
        tract_source.reshape(1, 128),
        tract_delay.reshape(1, 128),
        tract_target,
        tract_block.reshape(1, 128),
        tract_weight.reshape(1, 128),
        voxel_owner.reshape(32, 128),
        vaso_signal,
        blood_flow,
    )


def planned(*args):
    shapes = (
        lax.axis_size("patch"),
        lax.axis_size("trial"),
        args[0].shape,
        args[7].shape,
        args[13].shape,
    )
    if shapes == (8, 4, (8, 4096), (128,), (8, 128)):
        return fused(*args)
    return shards(*args)


def solution(mesh):
    placed = (
        P("trial", "patch"),
        P(None, "trial", "patch"),
        P("patch"),
        P("trial"),
        P("trial"),
        P("patch", "trial", None, None),
        P("patch", None),
        P("patch"),
        P("patch"),
        P("patch", None),
        P("patch"),
        P("patch"),
        P("patch"),
        P("trial", "patch"),
        P("trial", "patch"),
    )
    return jax.shard_map(
        planned,
        mesh=mesh,
        in_specs=placed,
        out_specs=(P("trial", "patch"), P("trial", "patch"), P("trial", "patch")),
        check_vma=False,
    )
```

```python
import functools

import jax
import jax.numpy as jnp
from jax import lax
from jax.experimental import pallas as pl
from jax.experimental.pallas import tpu as pltpu
from jax.sharding import PartitionSpec as P

BLOCK = 128
STEPS = 4
HIST = 7
CHUNKS = 8
MESH = pl.DeviceIdType.MESH


def extended_2(array, sides, width):
    for axis, dim in sides:
        peers, length = (lax.axis_size(axis), array.shape[dim])
        up = [(i, (i + 1) % peers) for i in range(peers - 1)]
        down = [(j, i) for i, j in up]
        last = lax.slice_in_dim(array, length - width, length, axis=dim)
        leading = lax.slice_in_dim(array, 0, width, axis=dim)
        before = lax.ppermute(last, axis, up)
        after = lax.ppermute(leading, axis, down)
        array = jnp.concatenate([before, array, after], axis=dim)
    return array


def shards(
    activity,
    history,
    drive,
    slope,
    strength,
    kernel,
    kernel_index,
    tract_source,
    tract_delay,
    tract_target,
    tract_block,
    tract_weight,
    voxel_owner,
    vaso_signal,
    blood_flow,
):
    trials_here = activity.shape[0]
    verts = activity.shape[1]
    nblk = verts // BLOCK
    patches = lax.axis_size("patch")
    tracts_here = tract_source.shape[0]
    capacity = max(2, tracts_here // patches + 1)
    slots = patches * capacity
    voxels_here = vaso_signal.shape[1]
    hist_blocks = history.reshape(HIST, trials_here, nblk, BLOCK)
    lag = tract_delay[:, None] - jnp.arange(STEPS, dtype=jnp.int32)[None, :] - 1
    rows = hist_blocks[lag, :, tract_source[:, None], :]
    weighted = (rows.astype(jnp.float32) * tract_weight[:, None, None, None]).astype(jnp.bfloat16)
    target = tract_target[:, 0]
    order = jnp.arange(tracts_here, dtype=jnp.int32)
    same = (target[:, None] == target[None, :]) & (order[None, :] < order[:, None])
    rank = jnp.sum(same.astype(jnp.int32), axis=1)
    slot = target * capacity + rank
    send_rates = jnp.zeros((slots, STEPS, trials_here, BLOCK), jnp.bfloat16).at[slot].set(weighted)
    send_blocks = jnp.full((slots,), -1, jnp.int32).at[slot].set(tract_block)
    got_rates, got_blocks = (
        lax.all_to_all(send_rates, "patch", split_axis=0, concat_axis=0, tiled=True),
        lax.all_to_all(send_blocks, "patch", split_axis=0, concat_axis=0, tiled=True),
    )
    onehot = (got_blocks[None, :] == jnp.arange(nblk, dtype=jnp.int32)[:, None]).astype(
        jnp.bfloat16
    )
    coupling = jnp.einsum("bs,sxtj->xtbj", onehot, got_rates, preferred_element_type=jnp.float32)
    coupling = coupling.reshape(STEPS, trials_here, verts)
    tiles = lax.all_gather(kernel, "trial", axis=1, tiled=True)
    rate = activity
    recorded = []
    for step in range(STEPS):
        rate_b = rate.astype(jnp.bfloat16)
        extended = extended_2(rate_b, (("patch", 1),), BLOCK)
        extended = extended.reshape(trials_here, nblk + 2, BLOCK)
        picked = extended[:, kernel_index]
        local = jnp.einsum("tbki,bkij->tbj", picked, tiles, preferred_element_type=jnp.float32)
        local = local.reshape(trials_here, verts)
        pre = slope[:, None] * (local + strength[:, None] * coupling[step] + drive[None, :])
        rate = rate + 0.5 * (jax.nn.sigmoid(pre) - rate)
        recorded.append(rate)
    values = jnp.concatenate(
        [
            jnp.stack(recorded).reshape(STEPS * trials_here, verts),
            jnp.ones((1, verts), jnp.float32),
        ],
        axis=0,
    )
    offset = (lax.axis_index("patch") - 1) * voxels_here
    partial_value = (
        jnp.zeros((values.shape[0], 3 * voxels_here), jnp.float32)
        .at[:, voxel_owner - offset]
        .add(values)
    )
    widened = extended_2(partial_value, (("patch", 1),), voxels_here)
    mine = (
        widened[:, :voxels_here]
        + widened[:, 2 * voxels_here : 3 * voxels_here]
        + widened[:, 4 * voxels_here :]
    )
    floor = jnp.maximum(mine[-1], 1.0)
    levels = mine[:-1].reshape(STEPS, trials_here, voxels_here) / floor[None, None, :]
    vaso = vaso_signal
    flow = blood_flow
    for step in range(STEPS):
        vaso = vaso + 0.5 * (levels[step] - 0.65 * vaso - 0.41 * (flow - 1.0))
        flow = flow + 0.5 * vaso
    return (rate, vaso, flow)


def window(
    patches,
    groups,
    act_hbm,
    hist_hbm,
    drive_ref,
    slope_ref,
    strength_ref,
    kern_ref,
    index_ref,
    source_ref,
    delay_ref,
    target_ref,
    block_ref,
    weight_ref,
    owner_ref,
    vaso_ref,
    flow_ref,
    act_out,
    vaso_out,
    flow_out,
    act_ref,
    hist_ref,
    ht,
    hist2,
    send,
    recv,
    over_f,
    over_send,
    over_recv,
    meta_send,
    meta_recv,
    tiles,
    ext0,
    ext1,
    ext2,
    ext3,
    ext4,
    halo_send,
    halo,
    coupling,
    owned,
    vox_send,
    vox,
    send_sem,
    recv_sem,
    osend_sem,
    orecv_sem,
    msend_sem,
    mrecv_sem,
    xsend_sem,
    xrecv_sem,
    rsend_sem,
    rrecv_sem,
    csem,
    hsend_sem,
    hrecv_sem,
    vsend_sem,
    vrecv_sem,
    local_sem,
):
    ext = (ext0, ext1, ext2, ext3, ext4)
    f32, bf16, i32 = jnp.float32, jnp.bfloat16, jnp.int32
    n = patches
    nblk = 32
    me = lax.axis_index("patch")
    grp = lax.axis_index("trial")
    far = lax.rem(grp + 2, groups)
    near = grp + 1 - 2 * lax.rem(grp, 2)

    barrier = pltpu.get_barrier_semaphore()
    for d in range(1, n):
        pl.semaphore_signal(
            barrier, inc=1, device_id={"patch": lax.rem(me + d, n)}, device_id_type=MESH
        )
    for g in (far, near):
        pl.semaphore_signal(barrier, inc=1, device_id={"trial": g}, device_id_type=MESH)

    def remote(src, dst, ssem, rsem, where):
        return pltpu.make_async_remote_copy(
            src_ref=src,
            dst_ref=dst,
            send_sem=ssem,
            recv_sem=rsem,
            device_id=where,
            device_id_type=MESH,
        )

    def part(c):
        return pl.ds(c * (nblk // CHUNKS), nblk // CHUNKS)

    own_history = pltpu.make_async_copy(hist_hbm, hist_ref, local_sem.at[1])
    own_history.start()
    own_activity = pltpu.make_async_copy(act_hbm, act_ref, local_sem.at[2])
    own_activity.start()
    own_tiles = pltpu.make_async_copy(kern_ref, tiles.at[grp], local_sem.at[0])
    own_tiles.start()

    def tile_far(k, c):
        return remote(
            kern_ref.at[part(c)],
            tiles.at[k, part(c)],
            xsend_sem.at[c],
            xrecv_sem.at[c],
            {"trial": far},
        )

    def tile_near(k):
        return remote(kern_ref, tiles.at[k], csem.at[0], csem.at[1], {"trial": near})

    def tile_relay(k, c):
        return remote(
            tiles.at[k, part(c)],
            tiles.at[k, part(c)],
            rsend_sem.at[c],
            rrecv_sem.at[c],
            {"trial": near},
        )

    def main_copy(s, p, q):
        return remote(
            send.at[s, pl.ds(pl.multiple_of(q * 16, 16), 16)],
            recv.at[s, pl.ds(pl.multiple_of(p * 16, 16), 16)],
            send_sem.at[s, q],
            recv_sem.at[s, p],
            {"patch": q},
        )

    def over_copy(p, q):
        return remote(
            over_send.at[q], over_recv.at[p], osend_sem.at[q], orecv_sem.at[p], {"patch": q}
        )

    def meta_copy(p, q):
        return remote(
            meta_send.at[q], meta_recv.at[p], msend_sem.at[q], mrecv_sem.at[p], {"patch": q}
        )

    def halo_copy(s, side):
        where = me + 1 if side == 0 else me - 1
        return remote(
            halo_send.at[s, side],
            halo.at[s, side],
            hsend_sem.at[s, side],
            hrecv_sem.at[s, side],
            {"patch": where},
        )

    def vox_copy(side):
        where = me + 1 if side == 0 else me - 1
        return remote(
            vox_send.at[side], vox.at[side], vsend_sem.at[side], vrecv_sem.at[side], {"patch": where}
        )

    has_left, has_right = me > 0, me < n - 1

    def halo_start(s):
        halo_send[s, 0] = ext[s][nblk]
        halo_send[s, 1] = ext[s][1]

        @pl.when(has_right)
        def _():
            halo_copy(s, 0).start()

        @pl.when(has_left)
        def _():
            halo_copy(s, 1).start()

    def halo_take(s):
        @pl.when(has_left)
        def _():
            halo_copy(s, 0).wait_recv()
            ext[s][0] = halo[s, 0]

        @pl.when(has_right)
        def _():
            halo_copy(s, 1).wait_recv()
            ext[s][nblk + 1] = halo[s, 1]

    sub = lax.broadcasted_iota(i32, (128, 128), 0)
    lane = lax.broadcasted_iota(i32, (128, 128), 1)
    eye = sub == lane

    target_row = target_ref[...].astype(f32)
    target_col = jnp.sum(jnp.where(eye, target_row, 0.0), axis=1, keepdims=True)
    same = target_col == target_row
    rank_row = jnp.sum(jnp.where(same & (sub < lane), 1.0, 0.0), axis=0, keepdims=True)
    rank_col = jnp.sum(jnp.where(same & (lane < sub), 1.0, 0.0), axis=1, keepdims=True)
    key_row = ((delay_ref[...] - 1) * nblk + source_ref[...]).astype(f32)
    weight_row = weight_ref[...]
    slot_row = jnp.where(rank_row < 16.0, target_row * 16.0 + rank_row, -1.0)
    sel = sub.astype(f32) == slot_row
    q8 = lax.broadcasted_iota(i32, (n, 128), 0).astype(f32)
    sel_over = (q8 == target_row) & (rank_row == 16.0)

    def pick(mask, row):
        return jnp.sum(jnp.where(mask, row, 0.0), axis=1, keepdims=True)

    key = pick(sel, key_row)
    weight = pick(sel, weight_row)
    key_over = pick(sel_over, key_row)
    weight_over = pick(sel_over, weight_row)

    def turn(lag, _):
        old = hist_ref[lag].astype(f32)
        for b in range(nblk):
            ht[lag, pl.ds(b, 8, stride=nblk), :] = old[:, b * 128 : (b + 1) * 128]
        rows = pl.ds(pl.multiple_of(lag * nblk, nblk), nblk)
        for j in range(8):
            hist2[rows, j * 128 : (j + 1) * 128] = ht[lag, j * nblk : (j + 1) * nblk, :].astype(bf16)
        return 0

    own_history.wait()
    lax.fori_loop(0, HIST, turn, 0)
    hist2[HIST * nblk :, :] = jnp.zeros((nblk, 1024), bf16)

    wide = lax.broadcasted_iota(i32, (128, 256), 1).astype(f32)
    wide8 = lax.broadcasted_iota(i32, (n, 256), 1).astype(f32)

    def gathered(s):
        choose = jnp.where(wide == key - float(s * nblk), 1.0, 0.0).astype(bf16)
        rows = jnp.dot(choose, hist2[...], preferred_element_type=f32)
        send[s] = (rows * weight).astype(bf16)

    gathered(0)

    a = jnp.where(q8 == target_row, block_ref[...].astype(f32), 0.0).astype(bf16)
    lanes = lane.astype(f32)
    mef = me.astype(f32)
    b1 = jnp.where((rank_col < 16.0) & (lanes == rank_col + mef * 16.0), 1.0, 0.0).astype(bf16)
    b2 = jnp.where((rank_col == 16.0) & (lanes == mef), 1.0, 0.0).astype(bf16)
    m1 = jnp.dot(a, b1, preferred_element_type=f32)
    m2 = jnp.dot(a, b2, preferred_element_type=f32)
    m = jnp.concatenate([m1, m2], axis=1)
    for q in range(n):
        meta_send[q] = jnp.broadcast_to(m[q : q + 1], (8, 256))

    own_activity.wait()
    for b in range(nblk):
        ext[0][b + 1] = act_ref[:, b * 128 : (b + 1) * 128]
    for s in range(STEPS):
        ext[s][0] = jnp.zeros((8, 128), f32)
        ext[s][nblk + 1] = jnp.zeros((8, 128), f32)

    pl.semaphore_wait(barrier, n + 1)
    for c in range(CHUNKS):
        tile_far(grp, c).start()
    for d in range(1, n):
        main_copy(0, me, lax.rem(me + d, n)).start()
    tile_near(grp).start()
    halo_start(0)
    for d in range(1, n):
        meta_copy(me, lax.rem(me + d, n)).start()
    for s in range(1, STEPS):
        gathered(s)
        for d in range(1, n):
            main_copy(s, me, lax.rem(me + d, n)).start()
        if s == 1:
            choose = jnp.concatenate(
                [jnp.where(wide8 == key_over - float(t * nblk), 1.0, 0.0) for t in range(STEPS)],
                axis=0,
            ).astype(bf16)
            rows = jnp.dot(choose, hist2[...], preferred_element_type=f32)
            for t in range(STEPS):
                for j in range(8):
                    over_f[pl.ds(t * 8 + j, n, stride=32), :] = (
                        rows[t * 8 : t * 8 + 8, j * 128 : (j + 1) * 128] * weight_over
                    )
            for q in range(n):
                over_send[q] = over_f[q * 32 : (q + 1) * 32, :].astype(bf16)
            for d in range(1, n):
                over_copy(me, lax.rem(me + d, n)).start()

    mine16 = pl.ds(pl.multiple_of(me * 16, 16), 16)
    for s in range(STEPS):
        recv[s, mine16, :] = send[s, mine16, :]
    over_recv[me] = over_send[me]
    meta_recv[me] = meta_send[me]

    first = ((me - 1) * 128).astype(f32)
    vox_id = lax.broadcasted_iota(i32, (384, 128), 0).astype(f32) + first

    def member(b, _):
        owner = owner_ref[pl.ds(b, 1), :].astype(f32)
        owned[b] = jnp.where(vox_id == owner, 1.0, 0.0).astype(bf16)
        return 0

    lax.fori_loop(0, nblk, member, 0)

    eye8 = lax.broadcasted_iota(i32, (8, 8), 0) == lax.broadcasted_iota(i32, (8, 8), 1)
    slope = jnp.sum(jnp.where(eye8, slope_ref[...], 0.0), axis=1, keepdims=True)
    strength = jnp.sum(jnp.where(eye8, strength_ref[...], 0.0), axis=1, keepdims=True)
    slope = jnp.broadcast_to(slope, (8, 128))
    strength = jnp.broadcast_to(strength, (8, 128))

    for d in range(1, n):
        p = lax.rem(me + d, n)
        meta_copy(p, me).wait_recv()
        over_copy(p, me).wait_recv()
    where_row = meta_recv[0]
    for p in range(1, n):
        where_row = where_row + meta_recv[p]
    where_row = where_row[0:1, 0:144]
    onehot = jnp.where(
        lax.broadcasted_iota(i32, (nblk, 144), 0).astype(f32) == where_row, 1.0, 0.0
    ).astype(bf16)
    for p in range(n):
        over_f[p * 32 : (p + 1) * 32, :] = over_recv[p].astype(f32)
    for s in range(STEPS):
        extra = jnp.concatenate(
            [over_f[pl.ds(s * 8 + j, n, stride=32), :] for j in range(8)], axis=1
        )
        recv[s, 128:144, :] = jnp.concatenate([extra, jnp.zeros_like(extra)], axis=0).astype(bf16)

    def couple(s):
        for d in range(1, n):
            main_copy(s, lax.rem(me + d, n), me).wait_recv()
        total = jnp.dot(onehot, recv[s], preferred_element_type=f32)
        for j in range(8):
            coupling[s, j * nblk : (j + 1) * nblk, :] = total[:, j * 128 : (j + 1) * 128]

    def update(s, blocks):
        rates = []
        for b in blocks:
            lhs = jnp.concatenate([ext[s][index_ref[k, b]] for k in range(4)], axis=1).astype(bf16)
            rhs = jnp.concatenate([tiles[k, b] for k in range(4)], axis=0)
            local = jnp.dot(lhs, rhs, preferred_element_type=f32)
            tract = coupling[s, pl.ds(b, 8, stride=nblk), :]
            pre = slope * (local + strength * tract + drive_ref[pl.ds(b, 1), :])
            rate = ext[s][b + 1]
            rates.append(rate + 0.5 * (jax.nn.sigmoid(pre) - rate))
        for b, rate in zip(blocks, rates):
            ext[s + 1][b + 1] = rate

    def updates(s, low, high, width):
        def some(i, _):
            update(s, [low + i * width + u for u in range(width)])
            return 0

        lax.fori_loop(0, (high - low) // width, some, 0)

    couple(0)
    halo_take(0)
    own_tiles.wait()
    tile_near(near).wait_recv()
    tile_far(far, 0).wait_recv()
    tile_relay(far, 0).start()
    other = lax.rem(near + 2, groups)
    for c in range(CHUNKS):
        if c + 1 < CHUNKS:
            tile_far(far, c + 1).wait_recv()
            tile_relay(far, c + 1).start()
        tile_relay(other, c).wait_recv()
        updates(0, c * (nblk // CHUNKS), (c + 1) * (nblk // CHUNKS), nblk // CHUNKS)
    halo_start(1)

    for s in range(1, STEPS):
        couple(s)
        updates(s, 1, nblk - 1, 15)
        halo_take(s)
        update(s, [0, nblk - 1])
        if s + 1 < STEPS:
            halo_start(s + 1)

    ones = jnp.ones((64, 512), bf16)

    def sums(i, total):
        rates = [
            jnp.concatenate([ext[s + 1][i * 4 + u + 1] for u in range(4)], axis=1)
            for s in range(STEPS)
        ]
        rates = jnp.concatenate(rates, axis=0)
        high = rates.astype(bf16)
        low = (rates - high.astype(f32)).astype(bf16)
        lhs = jnp.concatenate([high, low, ones], axis=0)
        rhs = jnp.concatenate([owned[i * 4 + u] for u in range(4)], axis=1)
        return total + lax.dot_general(
            rhs, lhs, (((1,), (1,)), ((), ())), preferred_element_type=f32
        )

    total = lax.fori_loop(0, nblk // 4, sums, jnp.zeros((384, 128), f32))
    total = total.T
    total = jnp.concatenate([total[0:32] + total[32:64], total[64:72]], axis=0)
    vox_send[0] = total[:, 256:384]
    vox_send[1] = total[:, 0:128]

    @pl.when(has_right)
    def _():
        vox_copy(0).start()

    @pl.when(has_left)
    def _():
        vox_copy(1).start()

    vox_send[2] = total[:, 128:256]
    for b in range(nblk):
        act_out[:, b * 128 : (b + 1) * 128] = ext[STEPS][b + 1]

    @pl.when(has_left)
    def _():
        vox_copy(0).wait_recv()
        vox_send[2] = vox_send[2] + vox[0]

    @pl.when(has_right)
    def _():
        vox_copy(1).wait_recv()
        vox_send[2] = vox_send[2] + vox[1]

    floor = jnp.maximum(vox_send[2, 32:40, :], 1.0)
    vaso = vaso_ref[...]
    flow = flow_ref[...]
    for s in range(STEPS):
        level = vox_send[2, s * 8 : s * 8 + 8, :] / floor
        vaso = vaso + 0.5 * (level - 0.65 * vaso - 0.41 * (flow - 1.0))
        flow = flow + 0.5 * vaso
    vaso_out[...] = vaso
    flow_out[...] = flow

    for d in range(1, n):
        q = lax.rem(me + d, n)
        for s in range(STEPS):
            main_copy(s, me, q).wait_send()
        over_copy(me, q).wait_send()
        meta_copy(me, q).wait_send()
    tile_near(grp).wait_send()
    for c in range(CHUNKS):
        tile_far(grp, c).wait_send()
        tile_relay(far, c).wait_send()

    @pl.when(has_right)
    def _():
        for s in range(STEPS):
            halo_copy(s, 0).wait_send()
        vox_copy(0).wait_send()

    @pl.when(has_left)
    def _():
        for s in range(STEPS):
            halo_copy(s, 1).wait_send()
        vox_copy(1).wait_send()


def fused(
    activity,
    history,
    drive,
    slope,
    strength,
    kernel,
    kernel_index,
    tract_source,
    tract_delay,
    tract_target,
    tract_block,
    tract_weight,
    voxel_owner,
    vaso_signal,
    blood_flow,
):
    n, groups = lax.axis_size("patch"), lax.axis_size("trial")
    f32, bf16 = jnp.float32, jnp.bfloat16
    vmem = pl.BlockSpec(memory_space=pltpu.VMEM)
    smem = pl.BlockSpec(memory_space=pltpu.SMEM)
    dma = pltpu.SemaphoreType.DMA
    hbm = pl.BlockSpec(memory_space=pltpu.HBM)
    scratch = [
        pltpu.VMEM(activity.shape, f32),
        pltpu.VMEM(history.shape, bf16),
        pltpu.VMEM((HIST, 256, 128), f32),
        pltpu.VMEM((256, 1024), bf16),
        pltpu.VMEM((STEPS, 128, 1024), bf16),
        pltpu.VMEM((STEPS, 144, 1024), bf16),
        pltpu.VMEM((256, 128), f32),
        pltpu.VMEM((n, 32, 128), bf16),
        pltpu.VMEM((n, 32, 128), bf16),
        pltpu.VMEM((n, 8, 256), f32),
        pltpu.VMEM((n, 8, 256), f32),
        pltpu.VMEM((4, 32, 128, 128), bf16),
        *[pltpu.VMEM((34, 8, 128), f32) for _ in range(STEPS + 1)],
        pltpu.VMEM((STEPS, 2, 8, 128), f32),
        pltpu.VMEM((STEPS, 2, 8, 128), f32),
        pltpu.VMEM((STEPS, 256, 128), f32),
        pltpu.VMEM((32, 384, 128), bf16),
        pltpu.VMEM((3, 40, 128), f32),
        pltpu.VMEM((2, 40, 128), f32),
        dma((STEPS, n)),
        dma((STEPS, n)),
        dma((n,)),
        dma((n,)),
        dma((n,)),
        dma((n,)),
        dma((CHUNKS,)),
        dma((CHUNKS,)),
        dma((CHUNKS,)),
        dma((CHUNKS,)),
        dma((2,)),
        dma((STEPS, 2)),
        dma((STEPS, 2)),
        dma((2,)),
        dma((2,)),
        dma((3,)),
    ]
    return pl.pallas_call(
        functools.partial(window, n, groups),
        out_shape=(
            jax.ShapeDtypeStruct(activity.shape, f32),
            jax.ShapeDtypeStruct(vaso_signal.shape, f32),
            jax.ShapeDtypeStruct(blood_flow.shape, f32),
        ),
        in_specs=[hbm] * 2 + [vmem] * 3 + [hbm, smem] + [vmem] * 8,
        out_specs=(vmem, vmem, vmem),
        scratch_shapes=scratch,
        compiler_params=pltpu.CompilerParams(
            collective_id=0, has_side_effects=True, vmem_limit_bytes=62 * 1024 * 1024
        ),
    )(
        activity,
        history,
        drive.reshape(32, 128),
        slope.reshape(1, 8),
        strength.reshape(1, 8),
        kernel.reshape(32, 128, 128),
        kernel_index.T,
        tract_source.reshape(1, 128),
        tract_delay.reshape(1, 128),
        tract_target.reshape(1, 128),
        tract_block.reshape(1, 128),
        tract_weight.reshape(1, 128),
        voxel_owner.reshape(32, 128),
        vaso_signal,
        blood_flow,
    )


def planned(*args):
    shapes = (
        lax.axis_size("patch"),
        lax.axis_size("trial"),
        args[0].shape,
        args[7].shape,
        args[13].shape,
    )
    if shapes == (8, 4, (8, 4096), (128,), (8, 128)):
        return fused(*args)
    return shards(*args)


def solution(mesh):
    placed = (
        P("trial", "patch"),
        P(None, "trial", "patch"),
        P("patch"),
        P("trial"),
        P("trial"),
        P("patch", "trial", None, None),
        P("patch", None),
        P("patch"),
        P("patch"),
        P("patch", None),
        P("patch"),
        P("patch"),
        P("patch"),
        P("trial", "patch"),
        P("trial", "patch"),
    )
    return jax.shard_map(
        planned,
        mesh=mesh,
        in_specs=placed,
        out_specs=(P("trial", "patch"), P("trial", "patch"), P("trial", "patch")),
        check_vma=False,
    )
```

```python
import functools

import jax
import jax.numpy as jnp
from jax import lax
from jax.experimental import pallas as pl
from jax.experimental.pallas import tpu as pltpu
from jax.sharding import PartitionSpec as P

BLOCK = 128
STEPS = 4
HIST = 7
STAGES = 4
MESH = pl.DeviceIdType.MESH


def extended_2(array, sides, width):
    for axis, dim in sides:
        peers, length = (lax.axis_size(axis), array.shape[dim])
        up = [(i, (i + 1) % peers) for i in range(peers - 1)]
        down = [(j, i) for i, j in up]
        last = lax.slice_in_dim(array, length - width, length, axis=dim)
        leading = lax.slice_in_dim(array, 0, width, axis=dim)
        before = lax.ppermute(last, axis, up)
        after = lax.ppermute(leading, axis, down)
        array = jnp.concatenate([before, array, after], axis=dim)
    return array


def shards(
    activity,
    history,
    drive,
    slope,
    strength,
    kernel,
    kernel_index,
    tract_source,
    tract_delay,
    tract_target,
    tract_block,
    tract_weight,
    voxel_owner,
    vaso_signal,
    blood_flow,
):
    trials_here = activity.shape[0]
    verts = activity.shape[1]
    nblk = verts // BLOCK
    patches = lax.axis_size("patch")
    tracts_here = tract_source.shape[0]
    capacity = max(2, tracts_here // patches + 1)
    slots = patches * capacity
    voxels_here = vaso_signal.shape[1]
    hist_blocks = history.reshape(HIST, trials_here, nblk, BLOCK)
    lag = tract_delay[:, None] - jnp.arange(STEPS, dtype=jnp.int32)[None, :] - 1
    rows = hist_blocks[lag, :, tract_source[:, None], :]
    weighted = (rows.astype(jnp.float32) * tract_weight[:, None, None, None]).astype(jnp.bfloat16)
    target = tract_target[:, 0]
    order = jnp.arange(tracts_here, dtype=jnp.int32)
    same = (target[:, None] == target[None, :]) & (order[None, :] < order[:, None])
    rank = jnp.sum(same.astype(jnp.int32), axis=1)
    slot = target * capacity + rank
    send_rates = jnp.zeros((slots, STEPS, trials_here, BLOCK), jnp.bfloat16).at[slot].set(weighted)
    send_blocks = jnp.full((slots,), -1, jnp.int32).at[slot].set(tract_block)
    got_rates, got_blocks = (
        lax.all_to_all(send_rates, "patch", split_axis=0, concat_axis=0, tiled=True),
        lax.all_to_all(send_blocks, "patch", split_axis=0, concat_axis=0, tiled=True),
    )
    onehot = (got_blocks[None, :] == jnp.arange(nblk, dtype=jnp.int32)[:, None]).astype(
        jnp.bfloat16
    )
    coupling = jnp.einsum("bs,sxtj->xtbj", onehot, got_rates, preferred_element_type=jnp.float32)
    coupling = coupling.reshape(STEPS, trials_here, verts)
    tiles = lax.all_gather(kernel, "trial", axis=1, tiled=True)
    rate = activity
    recorded = []
    for step in range(STEPS):
        rate_b = rate.astype(jnp.bfloat16)
        extended = extended_2(rate_b, (("patch", 1),), BLOCK)
        extended = extended.reshape(trials_here, nblk + 2, BLOCK)
        picked = extended[:, kernel_index]
        local = jnp.einsum("tbki,bkij->tbj", picked, tiles, preferred_element_type=jnp.float32)
        local = local.reshape(trials_here, verts)
        pre = slope[:, None] * (local + strength[:, None] * coupling[step] + drive[None, :])
        rate = rate + 0.5 * (jax.nn.sigmoid(pre) - rate)
        recorded.append(rate)
    values = jnp.concatenate(
        [
            jnp.stack(recorded).reshape(STEPS * trials_here, verts),
            jnp.ones((1, verts), jnp.float32),
        ],
        axis=0,
    )
    offset = (lax.axis_index("patch") - 1) * voxels_here
    partial_value = (
        jnp.zeros((values.shape[0], 3 * voxels_here), jnp.float32)
        .at[:, voxel_owner - offset]
        .add(values)
    )
    widened = extended_2(partial_value, (("patch", 1),), voxels_here)
    mine = (
        widened[:, :voxels_here]
        + widened[:, 2 * voxels_here : 3 * voxels_here]
        + widened[:, 4 * voxels_here :]
    )
    floor = jnp.maximum(mine[-1], 1.0)
    levels = mine[:-1].reshape(STEPS, trials_here, voxels_here) / floor[None, None, :]
    vaso = vaso_signal
    flow = blood_flow
    for step in range(STEPS):
        vaso = vaso + 0.5 * (levels[step] - 0.65 * vaso - 0.41 * (flow - 1.0))
        flow = flow + 0.5 * vaso
    return (rate, vaso, flow)


def window(
    patches,
    groups,
    act_hbm,
    hist_hbm,
    drive_ref,
    slope_ref,
    strength_ref,
    kern_ref,
    index_ref,
    source_ref,
    delay_ref,
    target_ref,
    block_ref,
    weight_ref,
    owner_ref,
    vaso_ref,
    flow_ref,
    act_out,
    vaso_out,
    flow_out,
    act_ref,
    hist_ref,
    ht,
    hist2,
    send,
    recv,
    over_f,
    over_send,
    over_recv,
    meta_send,
    meta_recv,
    tiles,
    ext0,
    ext1,
    ext2,
    ext3,
    ext4,
    halo_send,
    halo,
    coupling,
    owned,
    vox_send,
    vox,
    send_sem,
    recv_sem,
    osend_sem,
    orecv_sem,
    msend_sem,
    mrecv_sem,
    xsend_sem,
    xrecv_sem,
    rsend_sem,
    rrecv_sem,
    csem,
    hsend_sem,
    hrecv_sem,
    vsend_sem,
    vrecv_sem,
    local_sem,
):
    ext = (ext0, ext1, ext2, ext3, ext4)
    f32, bf16, i32 = jnp.float32, jnp.bfloat16, jnp.int32
    n = patches
    nblk = 32
    me = lax.axis_index("patch")
    grp = lax.axis_index("trial")
    far = lax.rem(grp + 2, groups)
    near = grp + 1 - 2 * lax.rem(grp, 2)

    barrier = pltpu.get_barrier_semaphore()
    for d in range(1, n):
        pl.semaphore_signal(
            barrier, inc=1, device_id={"patch": lax.rem(me + d, n)}, device_id_type=MESH
        )
    for g in (far, near):
        pl.semaphore_signal(barrier, inc=1, device_id={"trial": g}, device_id_type=MESH)

    def remote(src, dst, ssem, rsem, where):
        return pltpu.make_async_remote_copy(
            src_ref=src,
            dst_ref=dst,
            send_sem=ssem,
            recv_sem=rsem,
            device_id=where,
            device_id_type=MESH,
        )

    wide_part = nblk // (2 * STAGES)

    def part(m, side):
        low = m * wide_part if side == 0 else nblk - (m + 1) * wide_part
        return pl.ds(low, wide_part)

    own_history = pltpu.make_async_copy(hist_hbm, hist_ref, local_sem.at[1])
    own_history.start()
    own_activity = pltpu.make_async_copy(act_hbm, act_ref, local_sem.at[2])
    own_activity.start()
    own_tiles = pltpu.make_async_copy(kern_ref, tiles.at[grp], local_sem.at[0])
    own_tiles.start()

    def tile_far(k, m, side):
        return remote(
            kern_ref.at[part(m, side)],
            tiles.at[k, part(m, side)],
            xsend_sem.at[m, side],
            xrecv_sem.at[m, side],
            {"trial": far},
        )

    def tile_near(k):
        return remote(kern_ref, tiles.at[k], csem.at[0], csem.at[1], {"trial": near})

    def tile_relay(k, m, side):
        return remote(
            tiles.at[k, part(m, side)],
            tiles.at[k, part(m, side)],
            rsend_sem.at[m, side],
            rrecv_sem.at[m, side],
            {"trial": near},
        )

    def main_copy(s, p, q):
        return remote(
            send.at[s, pl.ds(pl.multiple_of(q * 16, 16), 16)],
            recv.at[s, pl.ds(pl.multiple_of(p * 16, 16), 16)],
            send_sem.at[s, q],
            recv_sem.at[s, p],
            {"patch": q},
        )

    def over_copy(p, q):
        return remote(
            over_send.at[q], over_recv.at[p], osend_sem.at[q], orecv_sem.at[p], {"patch": q}
        )

    def meta_copy(p, q):
        return remote(
            meta_send.at[q], meta_recv.at[p], msend_sem.at[q], mrecv_sem.at[p], {"patch": q}
        )

    def halo_copy(s, side):
        where = me + 1 if side == 0 else me - 1
        return remote(
            halo_send.at[s, side],
            halo.at[s, side],
            hsend_sem.at[s, side],
            hrecv_sem.at[s, side],
            {"patch": where},
        )

    def vox_copy(side):
        where = me + 1 if side == 0 else me - 1
        return remote(
            vox_send.at[side], vox.at[side], vsend_sem.at[side], vrecv_sem.at[side], {"patch": where}
        )

    has_left, has_right = me > 0, me < n - 1

    def halo_start(s):
        halo_send[s, 0] = ext[s][nblk]
        halo_send[s, 1] = ext[s][1]

        @pl.when(has_right)
        def _():
            halo_copy(s, 0).start()

        @pl.when(has_left)
        def _():
            halo_copy(s, 1).start()

    def halo_take(s):
        @pl.when(has_left)
        def _():
            halo_copy(s, 0).wait_recv()
            ext[s][0] = halo[s, 0]

        @pl.when(has_right)
        def _():
            halo_copy(s, 1).wait_recv()
            ext[s][nblk + 1] = halo[s, 1]

    sub = lax.broadcasted_iota(i32, (128, 128), 0)
    lane = lax.broadcasted_iota(i32, (128, 128), 1)
    eye = sub == lane

    target_row = target_ref[...].astype(f32)
    target_col = jnp.sum(jnp.where(eye, target_row, 0.0), axis=1, keepdims=True)
    same = target_col == target_row
    rank_row = jnp.sum(jnp.where(same & (sub < lane), 1.0, 0.0), axis=0, keepdims=True)
    rank_col = jnp.sum(jnp.where(same & (lane < sub), 1.0, 0.0), axis=1, keepdims=True)
    key_row = ((delay_ref[...] - 1) * nblk + source_ref[...]).astype(f32)
    weight_row = weight_ref[...]
    slot_row = jnp.where(rank_row < 16.0, target_row * 16.0 + rank_row, -1.0)
    sel = sub.astype(f32) == slot_row
    q8 = lax.broadcasted_iota(i32, (n, 128), 0).astype(f32)
    sel_over = (q8 == target_row) & (rank_row == 16.0)

    def pick(mask, row):
        return jnp.sum(jnp.where(mask, row, 0.0), axis=1, keepdims=True)

    key = pick(sel, key_row)
    weight = pick(sel, weight_row)
    key_over = pick(sel_over, key_row)
    weight_over = pick(sel_over, weight_row)

    def turn(lag, _):
        old = hist_ref[lag].astype(f32)
        for b in range(nblk):
            ht[lag, pl.ds(b, 8, stride=nblk), :] = old[:, b * 128 : (b + 1) * 128]
        rows = pl.ds(pl.multiple_of(lag * nblk, nblk), nblk)
        for j in range(8):
            hist2[rows, j * 128 : (j + 1) * 128] = ht[lag, j * nblk : (j + 1) * nblk, :].astype(bf16)
        return 0

    own_history.wait()
    lax.fori_loop(0, HIST, turn, 0)
    hist2[HIST * nblk :, :] = jnp.zeros((nblk, 1024), bf16)

    wide = lax.broadcasted_iota(i32, (128, 256), 1).astype(f32)
    wide8 = lax.broadcasted_iota(i32, (n, 256), 1).astype(f32)

    def gathered(s):
        choose = jnp.where(wide == key - float(s * nblk), 1.0, 0.0).astype(bf16)
        rows = jnp.dot(choose, hist2[...], preferred_element_type=f32)
        send[s] = (rows * weight).astype(bf16)

    gathered(0)

    a = jnp.where(q8 == target_row, block_ref[...].astype(f32), 0.0).astype(bf16)
    lanes = lane.astype(f32)
    mef = me.astype(f32)
    b1 = jnp.where((rank_col < 16.0) & (lanes == rank_col + mef * 16.0), 1.0, 0.0).astype(bf16)
    b2 = jnp.where((rank_col == 16.0) & (lanes == mef), 1.0, 0.0).astype(bf16)
    m1 = jnp.dot(a, b1, preferred_element_type=f32)
    m2 = jnp.dot(a, b2, preferred_element_type=f32)
    m = jnp.concatenate([m1, m2], axis=1)
    for q in range(n):
        meta_send[q] = jnp.broadcast_to(m[q : q + 1], (8, 256))

    own_activity.wait()
    for b in range(nblk):
        ext[0][b + 1] = act_ref[:, b * 128 : (b + 1) * 128]
    for s in range(STEPS):
        ext[s][0] = jnp.zeros((8, 128), f32)
        ext[s][nblk + 1] = jnp.zeros((8, 128), f32)

    pl.semaphore_wait(barrier, n + 1)
    def tiles_start(m):
        for side in range(2):
            tile_far(grp, m, side).start()

    def tracts_start(s):
        for d in range(1, n):
            main_copy(s, me, lax.rem(me + d, n)).start()

    tracts_start(0)
    tiles_start(0)
    tile_near(grp).start()
    halo_start(0)
    for d in range(1, n):
        meta_copy(me, lax.rem(me + d, n)).start()
    choose = jnp.concatenate(
        [jnp.where(wide8 == key_over - float(t * nblk), 1.0, 0.0) for t in range(STEPS)], axis=0
    ).astype(bf16)
    rows = jnp.dot(choose, hist2[...], preferred_element_type=f32)
    for t in range(STEPS):
        for j in range(8):
            over_f[pl.ds(t * 8 + j, n, stride=32), :] = (
                rows[t * 8 : t * 8 + 8, j * 128 : (j + 1) * 128] * weight_over
            )
    for q in range(n):
        over_send[q] = over_f[q * 32 : (q + 1) * 32, :].astype(bf16)
    for d in range(1, n):
        over_copy(me, lax.rem(me + d, n)).start()
    gathered(1)
    tracts_start(1)
    tiles_start(1)
    for s in range(2, STEPS):
        gathered(s)

    mine16 = pl.ds(pl.multiple_of(me * 16, 16), 16)
    for s in range(STEPS):
        recv[s, mine16, :] = send[s, mine16, :]
    over_recv[me] = over_send[me]
    meta_recv[me] = meta_send[me]

    first = ((me - 1) * 128).astype(f32)
    row_id = lax.broadcasted_iota(i32, (288, 128), 0)
    vox_id = (row_id + jnp.where(row_id >= 96, 32, 0) + jnp.where(row_id >= 192, 32, 0)).astype(f32)
    vox_id = vox_id + first

    def member(b, _):
        owner = owner_ref[pl.ds(b, 1), :].astype(f32)
        owned[b] = jnp.where(vox_id == owner, 1.0, 0.0).astype(bf16)
        return 0

    lax.fori_loop(0, nblk, member, 0)

    eye8 = lax.broadcasted_iota(i32, (8, 8), 0) == lax.broadcasted_iota(i32, (8, 8), 1)
    slope = jnp.sum(jnp.where(eye8, slope_ref[...], 0.0), axis=1, keepdims=True)
    strength = jnp.sum(jnp.where(eye8, strength_ref[...], 0.0), axis=1, keepdims=True)
    slope = jnp.broadcast_to(slope, (8, 128))
    strength = jnp.broadcast_to(strength, (8, 128))

    for d in range(1, n):
        p = lax.rem(me + d, n)
        meta_copy(p, me).wait_recv()
        over_copy(p, me).wait_recv()
    where_row = meta_recv[0]
    for p in range(1, n):
        where_row = where_row + meta_recv[p]
    where_row = where_row[0:1, 0:144]
    onehot = jnp.where(
        lax.broadcasted_iota(i32, (nblk, 144), 0).astype(f32) == where_row, 1.0, 0.0
    ).astype(bf16)
    for p in range(n):
        over_f[p * 32 : (p + 1) * 32, :] = over_recv[p].astype(f32)
    for s in range(STEPS):
        extra = jnp.concatenate(
            [over_f[pl.ds(s * 8 + j, n, stride=32), :] for j in range(8)], axis=1
        )
        recv[s, 128:144, :] = jnp.concatenate([extra, jnp.zeros_like(extra)], axis=0).astype(bf16)

    def couple(s):
        for d in range(1, n):
            main_copy(s, lax.rem(me + d, n), me).wait_recv()
        total = jnp.dot(onehot, recv[s], preferred_element_type=f32)
        for j in range(8):
            coupling[s, j * nblk : (j + 1) * nblk, :] = total[:, j * 128 : (j + 1) * 128]

    def update(s, blocks):
        rates = []
        for b in blocks:
            lhs = jnp.concatenate([ext[s][index_ref[k, b]] for k in range(4)], axis=1).astype(bf16)
            rhs = jnp.concatenate([tiles[k, b] for k in range(4)], axis=0)
            local = jnp.dot(lhs, rhs, preferred_element_type=f32)
            tract = coupling[s, pl.ds(b, 8, stride=nblk), :]
            pre = slope * (local + strength * tract + drive_ref[pl.ds(b, 1), :])
            rate = ext[s][b + 1]
            rates.append(rate + 0.5 * (jax.nn.sigmoid(pre) - rate))
        for b, rate in zip(blocks, rates):
            ext[s + 1][b + 1] = rate

    def region(s, m):
        if s > m:
            return set()
        reach = (m + 1) * wide_part - s
        if m == STAGES - 1:
            reach = nblk // 2
        return set(range(reach)) | set(range(nblk - reach, nblk))

    def step(s, m):
        todo = sorted(region(s, m) - (region(s, m - 1) if m > 0 else set()))
        for i in range(0, len(todo), 16):
            update(s, todo[i : i + 16])

    own_tiles.wait()
    tile_near(near).wait_recv()
    other = lax.rem(near + 2, groups)
    for m in range(STAGES):
        for side in range(2):
            tile_far(grp, m, side).wait_send()
        if m + 2 < STAGES:
            tiles_start(m + 2)
        for d in range(1, n):
            main_copy(m, me, lax.rem(me + d, n)).wait_send()
        if m + 2 < STEPS:
            tracts_start(m + 2)
        for side in range(2):
            tile_far(far, m, side).wait_recv()
            tile_relay(far, m, side).start()
        couple(m)
        for side in range(2):
            tile_relay(other, m, side).wait_recv()
        for s in range(m + 1):
            if s == m:
                halo_take(s)
            step(s, m)
            if s == m and s + 1 < STEPS:
                halo_start(s + 1)

    ones = jnp.ones((64, 512), bf16)

    def sums(i, total):
        rates = [
            jnp.concatenate([ext[s + 1][i * 4 + u + 1] for u in range(4)], axis=1)
            for s in range(STEPS)
        ]
        rates = jnp.concatenate(rates, axis=0)
        high = rates.astype(bf16)
        low = (rates - high.astype(f32)).astype(bf16)
        lhs = jnp.concatenate([high, low, ones], axis=0)
        rhs = jnp.concatenate([owned[i * 4 + u] for u in range(4)], axis=1)
        return total + lax.dot_general(
            rhs, lhs, (((1,), (1,)), ((), ())), preferred_element_type=f32
        )

    total = lax.fori_loop(0, nblk // 4, sums, jnp.zeros((288, 128), f32))

    def of_patch(i):
        rows = jnp.concatenate([total[i * 96 : (i + 1) * 96], jnp.zeros((32, 128), f32)], axis=0).T
        return jnp.concatenate([rows[0:32] + rows[32:64], rows[64:72]], axis=0)

    vox_send[0] = of_patch(2)
    vox_send[1] = of_patch(0)

    @pl.when(has_right)
    def _():
        vox_copy(0).start()

    @pl.when(has_left)
    def _():
        vox_copy(1).start()

    vox_send[2] = of_patch(1)
    for b in range(nblk):
        act_out[:, b * 128 : (b + 1) * 128] = ext[STEPS][b + 1]

    @pl.when(has_left)
    def _():
        vox_copy(0).wait_recv()
        vox_send[2] = vox_send[2] + vox[0]

    @pl.when(has_right)
    def _():
        vox_copy(1).wait_recv()
        vox_send[2] = vox_send[2] + vox[1]

    floor = jnp.maximum(vox_send[2, 32:40, :], 1.0)
    vaso = vaso_ref[...]
    flow = flow_ref[...]
    for s in range(STEPS):
        level = vox_send[2, s * 8 : s * 8 + 8, :] / floor
        vaso = vaso + 0.5 * (level - 0.65 * vaso - 0.41 * (flow - 1.0))
        flow = flow + 0.5 * vaso
    vaso_out[...] = vaso
    flow_out[...] = flow

    for d in range(1, n):
        q = lax.rem(me + d, n)
        over_copy(me, q).wait_send()
        meta_copy(me, q).wait_send()
    tile_near(grp).wait_send()
    for m in range(STAGES):
        for side in range(2):
            tile_relay(far, m, side).wait_send()

    @pl.when(has_right)
    def _():
        for s in range(STEPS):
            halo_copy(s, 0).wait_send()
        vox_copy(0).wait_send()

    @pl.when(has_left)
    def _():
        for s in range(STEPS):
            halo_copy(s, 1).wait_send()
        vox_copy(1).wait_send()


def hand_on(a, b, c, a_out, b_out, c_out, sems):
    copies = [
        pltpu.make_async_copy(src, dst, sems.at[i])
        for i, (src, dst) in enumerate(((a, a_out), (b, b_out), (c, c_out)))
    ]
    for copy in copies:
        copy.start()
    for copy in copies:
        copy.wait()


def fused(
    activity,
    history,
    drive,
    slope,
    strength,
    kernel,
    kernel_index,
    tract_source,
    tract_delay,
    tract_target,
    tract_block,
    tract_weight,
    voxel_owner,
    vaso_signal,
    blood_flow,
):
    n, groups = lax.axis_size("patch"), lax.axis_size("trial")
    f32, bf16 = jnp.float32, jnp.bfloat16
    vmem = pl.BlockSpec(memory_space=pltpu.VMEM)
    smem = pl.BlockSpec(memory_space=pltpu.SMEM)
    dma = pltpu.SemaphoreType.DMA
    hbm = pl.BlockSpec(memory_space=pltpu.HBM)
    scratch = [
        pltpu.VMEM(activity.shape, f32),
        pltpu.VMEM(history.shape, bf16),
        pltpu.VMEM((HIST, 256, 128), f32),
        pltpu.VMEM((256, 1024), bf16),
        pltpu.VMEM((STEPS, 128, 1024), bf16),
        pltpu.VMEM((STEPS, 144, 1024), bf16),
        pltpu.VMEM((256, 128), f32),
        pltpu.VMEM((n, 32, 128), bf16),
        pltpu.VMEM((n, 32, 128), bf16),
        pltpu.VMEM((n, 8, 256), f32),
        pltpu.VMEM((n, 8, 256), f32),
        pltpu.VMEM((4, 32, 128, 128), bf16),
        *[pltpu.VMEM((34, 8, 128), f32) for _ in range(STEPS + 1)],
        pltpu.VMEM((STEPS, 2, 8, 128), f32),
        pltpu.VMEM((STEPS, 2, 8, 128), f32),
        pltpu.VMEM((STEPS, 256, 128), f32),
        pltpu.VMEM((32, 288, 128), bf16),
        pltpu.VMEM((3, 40, 128), f32),
        pltpu.VMEM((2, 40, 128), f32),
        dma((STEPS, n)),
        dma((STEPS, n)),
        dma((n,)),
        dma((n,)),
        dma((n,)),
        dma((n,)),
        dma((STAGES, 2)),
        dma((STAGES, 2)),
        dma((STAGES, 2)),
        dma((STAGES, 2)),
        dma((2,)),
        dma((STEPS, 2)),
        dma((STEPS, 2)),
        dma((2,)),
        dma((2,)),
        dma((3,)),
    ]
    results = pl.pallas_call(
        functools.partial(window, n, groups),
        out_shape=(
            jax.ShapeDtypeStruct(activity.shape, f32),
            jax.ShapeDtypeStruct(vaso_signal.shape, f32),
            jax.ShapeDtypeStruct(blood_flow.shape, f32),
        ),
        in_specs=[hbm] * 2 + [vmem] * 3 + [hbm, smem] + [vmem] * 8,
        out_specs=(vmem, vmem, vmem),
        scratch_shapes=scratch,
        compiler_params=pltpu.CompilerParams(
            collective_id=0, has_side_effects=True, vmem_limit_bytes=62 * 1024 * 1024
        ),
    )(
        activity,
        history,
        drive.reshape(32, 128),
        slope.reshape(1, 8),
        strength.reshape(1, 8),
        kernel.reshape(32, 128, 128),
        kernel_index.T,
        tract_source.reshape(1, 128),
        tract_delay.reshape(1, 128),
        tract_target.reshape(1, 128),
        tract_block.reshape(1, 128),
        tract_weight.reshape(1, 128),
        voxel_owner.reshape(32, 128),
        vaso_signal,
        blood_flow,
    )
    return pl.pallas_call(
        hand_on,
        out_shape=tuple(jax.ShapeDtypeStruct(r.shape, r.dtype) for r in results),
        in_specs=[hbm] * 3,
        out_specs=(hbm, hbm, hbm),
        scratch_shapes=[dma((3,))],
        compiler_params=pltpu.CompilerParams(vmem_limit_bytes=62 * 1024 * 1024),
    )(*results)


def planned(*args):
    shapes = (
        lax.axis_size("patch"),
        lax.axis_size("trial"),
        args[0].shape,
        args[7].shape,
        args[13].shape,
    )
    if shapes == (8, 4, (8, 4096), (128,), (8, 128)):
        return fused(*args)
    return shards(*args)


def solution(mesh):
    placed = (
        P("trial", "patch"),
        P(None, "trial", "patch"),
        P("patch"),
        P("trial"),
        P("trial"),
        P("patch", "trial", None, None),
        P("patch", None),
        P("patch"),
        P("patch"),
        P("patch", None),
        P("patch"),
        P("patch"),
        P("patch"),
        P("trial", "patch"),
        P("trial", "patch"),
    )
    return jax.shard_map(
        planned,
        mesh=mesh,
        in_specs=placed,
        out_specs=(P("trial", "patch"), P("trial", "patch"), P("trial", "patch")),
        check_vma=False,
    )
```

```python
import functools

import jax
import jax.numpy as jnp
from jax import lax
from jax.experimental import pallas as pl
from jax.experimental.pallas import tpu as pltpu
from jax.sharding import PartitionSpec as P

BLOCK = 128
STEPS = 4
HIST = 7
STAGES = 4
MESH = pl.DeviceIdType.MESH


def extended_2(array, sides, width):
    for axis, dim in sides:
        peers, length = (lax.axis_size(axis), array.shape[dim])
        up = [(i, (i + 1) % peers) for i in range(peers - 1)]
        down = [(j, i) for i, j in up]
        last = lax.slice_in_dim(array, length - width, length, axis=dim)
        leading = lax.slice_in_dim(array, 0, width, axis=dim)
        before = lax.ppermute(last, axis, up)
        after = lax.ppermute(leading, axis, down)
        array = jnp.concatenate([before, array, after], axis=dim)
    return array


def shards(
    activity,
    history,
    drive,
    slope,
    strength,
    kernel,
    kernel_index,
    tract_source,
    tract_delay,
    tract_target,
    tract_block,
    tract_weight,
    voxel_owner,
    vaso_signal,
    blood_flow,
):
    trials_here = activity.shape[0]
    verts = activity.shape[1]
    nblk = verts // BLOCK
    patches = lax.axis_size("patch")
    tracts_here = tract_source.shape[0]
    capacity = max(2, tracts_here // patches + 1)
    slots = patches * capacity
    voxels_here = vaso_signal.shape[1]
    hist_blocks = history.reshape(HIST, trials_here, nblk, BLOCK)
    lag = tract_delay[:, None] - jnp.arange(STEPS, dtype=jnp.int32)[None, :] - 1
    rows = hist_blocks[lag, :, tract_source[:, None], :]
    weighted = (rows.astype(jnp.float32) * tract_weight[:, None, None, None]).astype(jnp.bfloat16)
    target = tract_target[:, 0]
    order = jnp.arange(tracts_here, dtype=jnp.int32)
    same = (target[:, None] == target[None, :]) & (order[None, :] < order[:, None])
    rank = jnp.sum(same.astype(jnp.int32), axis=1)
    slot = target * capacity + rank
    send_rates = jnp.zeros((slots, STEPS, trials_here, BLOCK), jnp.bfloat16).at[slot].set(weighted)
    send_blocks = jnp.full((slots,), -1, jnp.int32).at[slot].set(tract_block)
    got_rates, got_blocks = (
        lax.all_to_all(send_rates, "patch", split_axis=0, concat_axis=0, tiled=True),
        lax.all_to_all(send_blocks, "patch", split_axis=0, concat_axis=0, tiled=True),
    )
    onehot = (got_blocks[None, :] == jnp.arange(nblk, dtype=jnp.int32)[:, None]).astype(
        jnp.bfloat16
    )
    coupling = jnp.einsum("bs,sxtj->xtbj", onehot, got_rates, preferred_element_type=jnp.float32)
    coupling = coupling.reshape(STEPS, trials_here, verts)
    tiles = lax.all_gather(kernel, "trial", axis=1, tiled=True)
    rate = activity
    recorded = []
    for step in range(STEPS):
        rate_b = rate.astype(jnp.bfloat16)
        extended = extended_2(rate_b, (("patch", 1),), BLOCK)
        extended = extended.reshape(trials_here, nblk + 2, BLOCK)
        picked = extended[:, kernel_index]
        local = jnp.einsum("tbki,bkij->tbj", picked, tiles, preferred_element_type=jnp.float32)
        local = local.reshape(trials_here, verts)
        pre = slope[:, None] * (local + strength[:, None] * coupling[step] + drive[None, :])
        rate = rate + 0.5 * (jax.nn.sigmoid(pre) - rate)
        recorded.append(rate)
    values = jnp.concatenate(
        [
            jnp.stack(recorded).reshape(STEPS * trials_here, verts),
            jnp.ones((1, verts), jnp.float32),
        ],
        axis=0,
    )
    offset = (lax.axis_index("patch") - 1) * voxels_here
    partial_value = (
        jnp.zeros((values.shape[0], 3 * voxels_here), jnp.float32)
        .at[:, voxel_owner - offset]
        .add(values)
    )
    widened = extended_2(partial_value, (("patch", 1),), voxels_here)
    mine = (
        widened[:, :voxels_here]
        + widened[:, 2 * voxels_here : 3 * voxels_here]
        + widened[:, 4 * voxels_here :]
    )
    floor = jnp.maximum(mine[-1], 1.0)
    levels = mine[:-1].reshape(STEPS, trials_here, voxels_here) / floor[None, None, :]
    vaso = vaso_signal
    flow = blood_flow
    for step in range(STEPS):
        vaso = vaso + 0.5 * (levels[step] - 0.65 * vaso - 0.41 * (flow - 1.0))
        flow = flow + 0.5 * vaso
    return (rate, vaso, flow)


def window(
    patches,
    groups,
    act_hbm,
    hist_hbm,
    drive_ref,
    slope_ref,
    strength_ref,
    kern_ref,
    index_ref,
    source_ref,
    delay_ref,
    target_ref,
    block_ref,
    weight_ref,
    owner_ref,
    vaso_ref,
    flow_ref,
    act_out,
    vaso_out,
    flow_out,
    act_ref,
    hist_ref,
    ht,
    hist2,
    send,
    recv,
    over_f,
    over_send,
    over_recv,
    meta_send,
    meta_recv,
    tiles,
    ext0,
    ext1,
    ext2,
    ext3,
    ext4,
    halo_send,
    halo,
    coupling,
    owned,
    vox_send,
    vox,
    send_sem,
    recv_sem,
    osend_sem,
    orecv_sem,
    msend_sem,
    mrecv_sem,
    xsend_sem,
    xrecv_sem,
    rsend_sem,
    rrecv_sem,
    csem,
    hsend_sem,
    hrecv_sem,
    vsend_sem,
    vrecv_sem,
    local_sem,
):
    ext = (ext0, ext1, ext2, ext3, ext4)
    f32, bf16, i32 = jnp.float32, jnp.bfloat16, jnp.int32
    n = patches
    nblk = 32
    me = lax.axis_index("patch")
    grp = lax.axis_index("trial")
    far = lax.rem(grp + 2, groups)
    near = grp + 1 - 2 * lax.rem(grp, 2)

    barrier = pltpu.get_barrier_semaphore()
    for d in range(1, n):
        pl.semaphore_signal(
            barrier, inc=1, device_id={"patch": lax.rem(me + d, n)}, device_id_type=MESH
        )
    for g in (far, near):
        pl.semaphore_signal(barrier, inc=1, device_id={"trial": g}, device_id_type=MESH)

    def remote(src, dst, ssem, rsem, where):
        return pltpu.make_async_remote_copy(
            src_ref=src,
            dst_ref=dst,
            send_sem=ssem,
            recv_sem=rsem,
            device_id=where,
            device_id_type=MESH,
        )

    wide_part = nblk // (2 * STAGES)

    def part(m, side):
        low = m * wide_part if side == 0 else nblk - (m + 1) * wide_part
        return pl.ds(low, wide_part)

    own_history = pltpu.make_async_copy(hist_hbm, hist_ref, local_sem.at[1])
    own_history.start()
    own_activity = pltpu.make_async_copy(act_hbm, act_ref, local_sem.at[2])
    own_activity.start()
    own_tiles = pltpu.make_async_copy(kern_ref, tiles.at[grp], local_sem.at[0])
    own_tiles.start()

    def tile_far(k, m, side):
        return remote(
            kern_ref.at[part(m, side)],
            tiles.at[k, part(m, side)],
            xsend_sem.at[m, side],
            xrecv_sem.at[m, side],
            {"trial": far},
        )

    def tile_near(k):
        return remote(kern_ref, tiles.at[k], csem.at[0], csem.at[1], {"trial": near})

    def tile_relay(k, m, side):
        return remote(
            tiles.at[k, part(m, side)],
            tiles.at[k, part(m, side)],
            rsend_sem.at[m, side],
            rrecv_sem.at[m, side],
            {"trial": near},
        )

    def main_copy(s, p, q):
        return remote(
            send.at[s, pl.ds(pl.multiple_of(q * 16, 16), 16)],
            recv.at[s, pl.ds(pl.multiple_of(p * 16, 16), 16)],
            send_sem.at[s, q],
            recv_sem.at[s, p],
            {"patch": q},
        )

    def over_copy(p, q):
        return remote(
            over_send.at[q], over_recv.at[p], osend_sem.at[q], orecv_sem.at[p], {"patch": q}
        )

    def meta_copy(p, q):
        return remote(
            meta_send.at[q], meta_recv.at[p], msend_sem.at[q], mrecv_sem.at[p], {"patch": q}
        )

    def halo_copy(s, side):
        where = me + 1 if side == 0 else me - 1
        return remote(
            halo_send.at[s, side],
            halo.at[s, side],
            hsend_sem.at[s, side],
            hrecv_sem.at[s, side],
            {"patch": where},
        )

    def vox_copy(side):
        where = me + 1 if side == 0 else me - 1
        return remote(
            vox_send.at[side], vox.at[side], vsend_sem.at[side], vrecv_sem.at[side], {"patch": where}
        )

    has_left, has_right = me > 0, me < n - 1

    def halo_start(s):
        halo_send[s, 0] = ext[s][nblk]
        halo_send[s, 1] = ext[s][1]

        @pl.when(has_right)
        def _():
            halo_copy(s, 0).start()

        @pl.when(has_left)
        def _():
            halo_copy(s, 1).start()

    def halo_take(s):
        @pl.when(has_left)
        def _():
            halo_copy(s, 0).wait_recv()
            ext[s][0] = halo[s, 0]

        @pl.when(has_right)
        def _():
            halo_copy(s, 1).wait_recv()
            ext[s][nblk + 1] = halo[s, 1]

    sub = lax.broadcasted_iota(i32, (128, 128), 0)
    lane = lax.broadcasted_iota(i32, (128, 128), 1)
    eye = sub == lane
    lanes = lane.astype(f32)

    target_row = target_ref[...].astype(f32)
    target_col = jnp.sum(jnp.where(eye, target_row, 0.0), axis=1, keepdims=True)
    same = target_col == target_row
    rank_row = jnp.sum(jnp.where(same & (sub < lane), 1.0, 0.0), axis=0, keepdims=True)
    rank_col = jnp.sum(jnp.where(same & (lane < sub), 1.0, 0.0), axis=1, keepdims=True)
    key_row = ((delay_ref[...] - STEPS) * nblk + source_ref[...]).astype(f32)
    weight_row = weight_ref[...]
    slot_row = jnp.where(rank_row < 16.0, target_row * 16.0 + rank_row, -1.0)
    sel = sub.astype(f32) == slot_row
    q8 = lax.broadcasted_iota(i32, (n, 128), 0).astype(f32)
    sel_over = (q8 == target_row) & (rank_row == 16.0)

    def pick(mask, row):
        return jnp.sum(jnp.where(mask, row, 0.0), axis=1, keepdims=True)

    key = pick(sel, key_row)
    weight = pick(sel, weight_row)
    key_over = pick(sel_over, key_row)
    weight_over = pick(sel_over, weight_row)

    def turn(lag, _):
        old = hist_ref[lag].astype(f32)
        for b in range(nblk):
            ht[lag, pl.ds(b, 8, stride=nblk), :] = old[:, b * 128 : (b + 1) * 128]
        rows = pl.ds(pl.multiple_of(lag * nblk, nblk), nblk)
        for j in range(8):
            hist2[rows, j * 128 : (j + 1) * 128] = ht[lag, j * nblk : (j + 1) * nblk, :].astype(bf16)
        return 0

    def tiles_start(m):
        for side in range(2):
            tile_far(grp, m, side).start()

    def tracts_start(s):
        for d in range(1, n):
            main_copy(s, me, lax.rem(me + d, n)).start()

    pl.semaphore_wait(barrier, n + 1)
    tiles_start(0)
    tile_near(grp).start()

    choose = jnp.where(lanes == key, 1.0, 0.0).astype(bf16)

    def gathered(s):
        low = (STEPS - 1 - s) * nblk
        rows = jnp.dot(choose, hist2[low : low + 128, :], preferred_element_type=f32)
        send[s] = (rows * weight).astype(bf16)

    own_history.wait()
    lax.fori_loop(STEPS - 1, HIST, turn, 0)
    gathered(0)
    tracts_start(0)

    a = jnp.where(q8 == target_row, block_ref[...].astype(f32), 0.0).astype(bf16)
    mef = me.astype(f32)
    b1 = jnp.where((rank_col < 16.0) & (lanes == rank_col + mef * 16.0), 1.0, 0.0).astype(bf16)
    b2 = jnp.where((rank_col == 16.0) & (lanes == mef), 1.0, 0.0).astype(bf16)
    m1 = jnp.dot(a, b1, preferred_element_type=f32)
    m2 = jnp.dot(a, b2, preferred_element_type=f32)
    m = jnp.concatenate([m1, m2], axis=1)
    for q in range(n):
        meta_send[q] = jnp.broadcast_to(m[q : q + 1], (8, 256))

    own_activity.wait()
    for b in range(nblk):
        ext[0][b + 1] = act_ref[:, b * 128 : (b + 1) * 128]
    for s in range(STEPS):
        ext[s][0] = jnp.zeros((8, 128), f32)
        ext[s][nblk + 1] = jnp.zeros((8, 128), f32)

    halo_start(0)
    for d in range(1, n):
        meta_copy(me, lax.rem(me + d, n)).start()
    lax.fori_loop(0, STEPS - 1, turn, 0)
    gathered(1)
    tracts_start(1)
    tiles_start(1)
    choose_over = jnp.where(lanes[0:n] == key_over, 1.0, 0.0).astype(bf16)
    for t in range(STEPS):
        low = (STEPS - 1 - t) * nblk
        rows = jnp.dot(choose_over, hist2[low : low + 128, :], preferred_element_type=f32)
        for j in range(8):
            over_f[pl.ds(t * 8 + j, n, stride=32), :] = (
                rows[:, j * 128 : (j + 1) * 128] * weight_over
            )
    for q in range(n):
        over_send[q] = over_f[q * 32 : (q + 1) * 32, :].astype(bf16)
    for d in range(1, n):
        over_copy(me, lax.rem(me + d, n)).start()
    for s in range(2, STEPS):
        gathered(s)

    mine16 = pl.ds(pl.multiple_of(me * 16, 16), 16)
    for s in range(STEPS):
        recv[s, mine16, :] = send[s, mine16, :]
    over_recv[me] = over_send[me]
    meta_recv[me] = meta_send[me]

    first = ((me - 1) * 128).astype(f32)
    row_id = lax.broadcasted_iota(i32, (288, 128), 0)
    vox_id = (row_id + jnp.where(row_id >= 96, 32, 0) + jnp.where(row_id >= 192, 32, 0)).astype(f32)
    vox_id = vox_id + first

    def member(b, _):
        owner = owner_ref[pl.ds(b, 1), :].astype(f32)
        owned[b] = jnp.where(vox_id == owner, 1.0, 0.0).astype(bf16)
        return 0

    lax.fori_loop(0, nblk, member, 0)

    eye8 = lax.broadcasted_iota(i32, (8, 8), 0) == lax.broadcasted_iota(i32, (8, 8), 1)
    slope = jnp.sum(jnp.where(eye8, slope_ref[...], 0.0), axis=1, keepdims=True)
    strength = jnp.sum(jnp.where(eye8, strength_ref[...], 0.0), axis=1, keepdims=True)
    slope = jnp.broadcast_to(slope, (8, 128))
    strength = jnp.broadcast_to(strength, (8, 128))

    for d in range(1, n):
        p = lax.rem(me + d, n)
        meta_copy(p, me).wait_recv()
        over_copy(p, me).wait_recv()
    where_row = meta_recv[0]
    for p in range(1, n):
        where_row = where_row + meta_recv[p]
    where_row = where_row[0:1, 0:144]
    onehot = jnp.where(
        lax.broadcasted_iota(i32, (nblk, 144), 0).astype(f32) == where_row, 1.0, 0.0
    ).astype(bf16)
    for p in range(n):
        over_f[p * 32 : (p + 1) * 32, :] = over_recv[p].astype(f32)
    for s in range(STEPS):
        extra = jnp.concatenate(
            [over_f[pl.ds(s * 8 + j, n, stride=32), :] for j in range(8)], axis=1
        )
        recv[s, 128:144, :] = jnp.concatenate([extra, jnp.zeros_like(extra)], axis=0).astype(bf16)

    def couple(s):
        for d in range(1, n):
            main_copy(s, lax.rem(me + d, n), me).wait_recv()
        total = jnp.dot(onehot, recv[s], preferred_element_type=f32)
        for j in range(8):
            coupling[s, j * nblk : (j + 1) * nblk, :] = total[:, j * 128 : (j + 1) * 128]

    def update(s, blocks):
        rates = []
        for b in blocks:
            lhs = jnp.concatenate([ext[s][index_ref[k, b]] for k in range(4)], axis=1).astype(bf16)
            rhs = jnp.concatenate([tiles[k, b] for k in range(4)], axis=0)
            local = jnp.dot(lhs, rhs, preferred_element_type=f32)
            tract = coupling[s, pl.ds(b, 8, stride=nblk), :]
            pre = slope * (local + strength * tract + drive_ref[pl.ds(b, 1), :])
            rate = ext[s][b + 1]
            rates.append(rate + 0.5 * (jax.nn.sigmoid(pre) - rate))
        for b, rate in zip(blocks, rates):
            ext[s + 1][b + 1] = rate

    def region(s, m):
        if s > m:
            return set()
        reach = (m + 1) * wide_part - s
        if m == STAGES - 1:
            reach = nblk // 2
        return set(range(reach)) | set(range(nblk - reach, nblk))

    def step(s, m):
        todo = sorted(region(s, m) - (region(s, m - 1) if m > 0 else set()))
        for i in range(0, len(todo), 16):
            update(s, todo[i : i + 16])

    own_tiles.wait()
    tile_near(near).wait_recv()
    other = lax.rem(near + 2, groups)
    for m in range(STAGES):
        for side in range(2):
            tile_far(grp, m, side).wait_send()
        if m + 2 < STAGES:
            tiles_start(m + 2)
        for d in range(1, n):
            main_copy(m, me, lax.rem(me + d, n)).wait_send()
        if m + 2 < STEPS:
            tracts_start(m + 2)
        for side in range(2):
            tile_far(far, m, side).wait_recv()
            tile_relay(far, m, side).start()
        couple(m)
        for side in range(2):
            tile_relay(other, m, side).wait_recv()
        for s in range(m + 1):
            if s == m:
                halo_take(s)
            step(s, m)
            if s == m and s + 1 < STEPS:
                halo_start(s + 1)

    ones = jnp.ones((64, 512), bf16)

    def sums(i, total):
        rates = [
            jnp.concatenate([ext[s + 1][i * 4 + u + 1] for u in range(4)], axis=1)
            for s in range(STEPS)
        ]
        rates = jnp.concatenate(rates, axis=0)
        high = rates.astype(bf16)
        low = (rates - high.astype(f32)).astype(bf16)
        lhs = jnp.concatenate([high, low, ones], axis=0)
        rhs = jnp.concatenate([owned[i * 4 + u] for u in range(4)], axis=1)
        return total + lax.dot_general(
            rhs, lhs, (((1,), (1,)), ((), ())), preferred_element_type=f32
        )

    total = jnp.zeros((288, 128), f32)
    for i in range(nblk // 4):
        total = sums(i, total)

    def of_patch(i):
        rows = jnp.concatenate([total[i * 96 : (i + 1) * 96], jnp.zeros((32, 128), f32)], axis=0).T
        return jnp.concatenate([rows[0:32] + rows[32:64], rows[64:72]], axis=0)

    vox_send[0] = of_patch(2)
    vox_send[1] = of_patch(0)

    @pl.when(has_right)
    def _():
        vox_copy(0).start()

    @pl.when(has_left)
    def _():
        vox_copy(1).start()

    vox_send[2] = of_patch(1)
    for b in range(nblk):
        act_out[:, b * 128 : (b + 1) * 128] = ext[STEPS][b + 1]

    @pl.when(has_left)
    def _():
        vox_copy(0).wait_recv()
        vox_send[2] = vox_send[2] + vox[0]

    @pl.when(has_right)
    def _():
        vox_copy(1).wait_recv()
        vox_send[2] = vox_send[2] + vox[1]

    floor = jnp.maximum(vox_send[2, 32:40, :], 1.0)
    vaso = vaso_ref[...]
    flow = flow_ref[...]
    for s in range(STEPS):
        level = vox_send[2, s * 8 : s * 8 + 8, :] / floor
        vaso = vaso + 0.5 * (level - 0.65 * vaso - 0.41 * (flow - 1.0))
        flow = flow + 0.5 * vaso
    vaso_out[...] = vaso
    flow_out[...] = flow

    for d in range(1, n):
        q = lax.rem(me + d, n)
        over_copy(me, q).wait_send()
        meta_copy(me, q).wait_send()
    tile_near(grp).wait_send()
    for m in range(STAGES):
        for side in range(2):
            tile_relay(far, m, side).wait_send()

    @pl.when(has_right)
    def _():
        for s in range(STEPS):
            halo_copy(s, 0).wait_send()
        vox_copy(0).wait_send()

    @pl.when(has_left)
    def _():
        for s in range(STEPS):
            halo_copy(s, 1).wait_send()
        vox_copy(1).wait_send()


def hand_on(a, b, c, a_out, b_out, c_out):
    a_out[...] = a[...]
    b_out[...] = b[...]
    c_out[...] = c[...]


def fused(
    activity,
    history,
    drive,
    slope,
    strength,
    kernel,
    kernel_index,
    tract_source,
    tract_delay,
    tract_target,
    tract_block,
    tract_weight,
    voxel_owner,
    vaso_signal,
    blood_flow,
):
    n, groups = lax.axis_size("patch"), lax.axis_size("trial")
    f32, bf16 = jnp.float32, jnp.bfloat16
    vmem = pl.BlockSpec(memory_space=pltpu.VMEM)
    smem = pl.BlockSpec(memory_space=pltpu.SMEM)
    dma = pltpu.SemaphoreType.DMA
    hbm = pl.BlockSpec(memory_space=pltpu.HBM)
    scratch = [
        pltpu.VMEM(activity.shape, f32),
        pltpu.VMEM(history.shape, bf16),
        pltpu.VMEM((HIST, 256, 128), f32),
        pltpu.VMEM((HIST * 32, 1024), bf16),
        pltpu.VMEM((STEPS, 128, 1024), bf16),
        pltpu.VMEM((STEPS, 144, 1024), bf16),
        pltpu.VMEM((256, 128), f32),
        pltpu.VMEM((n, 32, 128), bf16),
        pltpu.VMEM((n, 32, 128), bf16),
        pltpu.VMEM((n, 8, 256), f32),
        pltpu.VMEM((n, 8, 256), f32),
        pltpu.VMEM((4, 32, 128, 128), bf16),
        *[pltpu.VMEM((34, 8, 128), f32) for _ in range(STEPS + 1)],
        pltpu.VMEM((STEPS, 2, 8, 128), f32),
        pltpu.VMEM((STEPS, 2, 8, 128), f32),
        pltpu.VMEM((STEPS, 256, 128), f32),
        pltpu.VMEM((32, 288, 128), bf16),
        pltpu.VMEM((3, 40, 128), f32),
        pltpu.VMEM((2, 40, 128), f32),
        dma((STEPS, n)),
        dma((STEPS, n)),
        dma((n,)),
        dma((n,)),
        dma((n,)),
        dma((n,)),
        dma((STAGES, 2)),
        dma((STAGES, 2)),
        dma((STAGES, 2)),
        dma((STAGES, 2)),
        dma((2,)),
        dma((STEPS, 2)),
        dma((STEPS, 2)),
        dma((2,)),
        dma((2,)),
        dma((3,)),
    ]
    results = pl.pallas_call(
        functools.partial(window, n, groups),
        out_shape=(
            jax.ShapeDtypeStruct(activity.shape, f32),
            jax.ShapeDtypeStruct(vaso_signal.shape, f32),
            jax.ShapeDtypeStruct(blood_flow.shape, f32),
        ),
        in_specs=[hbm] * 2 + [vmem] * 3 + [hbm, smem] + [vmem] * 8,
        out_specs=(vmem, vmem, vmem),
        scratch_shapes=scratch,
        compiler_params=pltpu.CompilerParams(
            collective_id=0, has_side_effects=True, vmem_limit_bytes=62 * 1024 * 1024
        ),
    )(
        activity,
        history,
        drive.reshape(32, 128),
        slope.reshape(1, 8),
        strength.reshape(1, 8),
        kernel.reshape(32, 128, 128),
        kernel_index.T,
        tract_source.reshape(1, 128),
        tract_delay.reshape(1, 128),
        tract_target.reshape(1, 128),
        tract_block.reshape(1, 128),
        tract_weight.reshape(1, 128),
        voxel_owner.reshape(32, 128),
        vaso_signal,
        blood_flow,
    )
    return pl.pallas_call(
        hand_on,
        out_shape=tuple(jax.ShapeDtypeStruct(r.shape, r.dtype) for r in results),
        in_specs=[vmem] * 3,
        out_specs=(vmem, vmem, vmem),
        compiler_params=pltpu.CompilerParams(vmem_limit_bytes=62 * 1024 * 1024),
    )(*results)


def planned(*args):
    shapes = (
        lax.axis_size("patch"),
        lax.axis_size("trial"),
        args[0].shape,
        args[7].shape,
        args[13].shape,
    )
    if shapes == (8, 4, (8, 4096), (128,), (8, 128)):
        return fused(*args)
    return shards(*args)


def solution(mesh):
    placed = (
        P("trial", "patch"),
        P(None, "trial", "patch"),
        P("patch"),
        P("trial"),
        P("trial"),
        P("patch", "trial", None, None),
        P("patch", None),
        P("patch"),
        P("patch"),
        P("patch", None),
        P("patch"),
        P("patch"),
        P("patch"),
        P("trial", "patch"),
        P("trial", "patch"),
    )
    return jax.shard_map(
        planned,
        mesh=mesh,
        in_specs=placed,
        out_specs=(P("trial", "patch"), P("trial", "patch"), P("trial", "patch")),
        check_vma=False,
    )
```

```python
import functools

import jax
import jax.numpy as jnp
from jax import lax
from jax.experimental import pallas as pl
from jax.experimental.pallas import tpu as pltpu
from jax.sharding import PartitionSpec as P

BLOCK = 128
STEPS = 4
HIST = 7
STAGES = 4
MESH = pl.DeviceIdType.MESH


def extended_2(array, sides, width):
    for axis, dim in sides:
        peers, length = (lax.axis_size(axis), array.shape[dim])
        up = [(i, (i + 1) % peers) for i in range(peers - 1)]
        down = [(j, i) for i, j in up]
        last = lax.slice_in_dim(array, length - width, length, axis=dim)
        leading = lax.slice_in_dim(array, 0, width, axis=dim)
        before = lax.ppermute(last, axis, up)
        after = lax.ppermute(leading, axis, down)
        array = jnp.concatenate([before, array, after], axis=dim)
    return array


def shards(
    activity,
    history,
    drive,
    slope,
    strength,
    kernel,
    kernel_index,
    tract_source,
    tract_delay,
    tract_target,
    tract_block,
    tract_weight,
    voxel_owner,
    vaso_signal,
    blood_flow,
):
    trials_here = activity.shape[0]
    verts = activity.shape[1]
    nblk = verts // BLOCK
    patches = lax.axis_size("patch")
    tracts_here = tract_source.shape[0]
    capacity = max(2, tracts_here // patches + 1)
    slots = patches * capacity
    voxels_here = vaso_signal.shape[1]
    hist_blocks = history.reshape(HIST, trials_here, nblk, BLOCK)
    lag = tract_delay[:, None] - jnp.arange(STEPS, dtype=jnp.int32)[None, :] - 1
    rows = hist_blocks[lag, :, tract_source[:, None], :]
    weighted = (rows.astype(jnp.float32) * tract_weight[:, None, None, None]).astype(jnp.bfloat16)
    target = tract_target[:, 0]
    order = jnp.arange(tracts_here, dtype=jnp.int32)
    same = (target[:, None] == target[None, :]) & (order[None, :] < order[:, None])
    rank = jnp.sum(same.astype(jnp.int32), axis=1)
    slot = target * capacity + rank
    send_rates = jnp.zeros((slots, STEPS, trials_here, BLOCK), jnp.bfloat16).at[slot].set(weighted)
    send_blocks = jnp.full((slots,), -1, jnp.int32).at[slot].set(tract_block)
    got_rates, got_blocks = (
        lax.all_to_all(send_rates, "patch", split_axis=0, concat_axis=0, tiled=True),
        lax.all_to_all(send_blocks, "patch", split_axis=0, concat_axis=0, tiled=True),
    )
    onehot = (got_blocks[None, :] == jnp.arange(nblk, dtype=jnp.int32)[:, None]).astype(
        jnp.bfloat16
    )
    coupling = jnp.einsum("bs,sxtj->xtbj", onehot, got_rates, preferred_element_type=jnp.float32)
    coupling = coupling.reshape(STEPS, trials_here, verts)
    tiles = lax.all_gather(kernel, "trial", axis=1, tiled=True)
    rate = activity
    recorded = []
    for step in range(STEPS):
        rate_b = rate.astype(jnp.bfloat16)
        extended = extended_2(rate_b, (("patch", 1),), BLOCK)
        extended = extended.reshape(trials_here, nblk + 2, BLOCK)
        picked = extended[:, kernel_index]
        local = jnp.einsum("tbki,bkij->tbj", picked, tiles, preferred_element_type=jnp.float32)
        local = local.reshape(trials_here, verts)
        pre = slope[:, None] * (local + strength[:, None] * coupling[step] + drive[None, :])
        rate = rate + 0.5 * (jax.nn.sigmoid(pre) - rate)
        recorded.append(rate)
    values = jnp.concatenate(
        [
            jnp.stack(recorded).reshape(STEPS * trials_here, verts),
            jnp.ones((1, verts), jnp.float32),
        ],
        axis=0,
    )
    offset = (lax.axis_index("patch") - 1) * voxels_here
    partial_value = (
        jnp.zeros((values.shape[0], 3 * voxels_here), jnp.float32)
        .at[:, voxel_owner - offset]
        .add(values)
    )
    widened = extended_2(partial_value, (("patch", 1),), voxels_here)
    mine = (
        widened[:, :voxels_here]
        + widened[:, 2 * voxels_here : 3 * voxels_here]
        + widened[:, 4 * voxels_here :]
    )
    floor = jnp.maximum(mine[-1], 1.0)
    levels = mine[:-1].reshape(STEPS, trials_here, voxels_here) / floor[None, None, :]
    vaso = vaso_signal
    flow = blood_flow
    for step in range(STEPS):
        vaso = vaso + 0.5 * (levels[step] - 0.65 * vaso - 0.41 * (flow - 1.0))
        flow = flow + 0.5 * vaso
    return (rate, vaso, flow)


def window(
    patches,
    groups,
    act_hbm,
    hist_hbm,
    drive_ref,
    slope_ref,
    strength_ref,
    kern_ref,
    index_ref,
    source_ref,
    delay_ref,
    target_ref,
    block_ref,
    weight_ref,
    owner_ref,
    vaso_ref,
    flow_ref,
    act_out,
    vaso_out,
    flow_out,
    act_ref,
    hist_ref,
    ht,
    hist2,
    send,
    recv,
    over_f,
    over_send,
    over_recv,
    meta_send,
    meta_recv,
    tiles,
    ext0,
    ext1,
    ext2,
    ext3,
    ext4,
    halo_send,
    halo,
    coupling,
    owned,
    vox_send,
    vox,
    send_sem,
    recv_sem,
    osend_sem,
    orecv_sem,
    msend_sem,
    mrecv_sem,
    xsend_sem,
    xrecv_sem,
    rsend_sem,
    rrecv_sem,
    csem,
    hsend_sem,
    hrecv_sem,
    vsend_sem,
    vrecv_sem,
    local_sem,
):
    ext = (ext0, ext1, ext2, ext3, ext4)
    f32, bf16, i32 = jnp.float32, jnp.bfloat16, jnp.int32
    n = patches
    nblk = 32
    me = lax.axis_index("patch")
    grp = lax.axis_index("trial")
    far = lax.rem(grp + 2, groups)
    near = grp + 1 - 2 * lax.rem(grp, 2)

    barrier = pltpu.get_barrier_semaphore()
    for d in range(1, n):
        pl.semaphore_signal(
            barrier, inc=1, device_id={"patch": lax.rem(me + d, n)}, device_id_type=MESH
        )
    for g in (far, near):
        pl.semaphore_signal(barrier, inc=1, device_id={"trial": g}, device_id_type=MESH)

    def remote(src, dst, ssem, rsem, where):
        return pltpu.make_async_remote_copy(
            src_ref=src,
            dst_ref=dst,
            send_sem=ssem,
            recv_sem=rsem,
            device_id=where,
            device_id_type=MESH,
        )

    wide_part = nblk // (2 * STAGES)

    def part(m, side):
        low = m * wide_part if side == 0 else nblk - (m + 1) * wide_part
        return pl.ds(low, wide_part)

    own_history = pltpu.make_async_copy(hist_hbm, hist_ref, local_sem.at[1])
    own_history.start()
    own_activity = pltpu.make_async_copy(act_hbm, act_ref, local_sem.at[2])
    own_activity.start()
    own_tiles = pltpu.make_async_copy(kern_ref, tiles.at[grp], local_sem.at[0])
    own_tiles.start()

    def tile_far(k, m, side):
        return remote(
            kern_ref.at[part(m, side)],
            tiles.at[k, part(m, side)],
            xsend_sem.at[m, side],
            xrecv_sem.at[m, side],
            {"trial": far},
        )

    def tile_near(k):
        return remote(kern_ref, tiles.at[k], csem.at[0], csem.at[1], {"trial": near})

    def tile_relay(k, m, side):
        return remote(
            tiles.at[k, part(m, side)],
            tiles.at[k, part(m, side)],
            rsend_sem.at[m, side],
            rrecv_sem.at[m, side],
            {"trial": near},
        )

    def main_copy(s, p, q):
        return remote(
            send.at[s, pl.ds(pl.multiple_of(q * 16, 16), 16)],
            recv.at[s, pl.ds(pl.multiple_of(p * 16, 16), 16)],
            send_sem.at[s, q],
            recv_sem.at[s, p],
            {"patch": q},
        )

    def over_copy(p, q):
        return remote(
            over_send.at[q], over_recv.at[p], osend_sem.at[q], orecv_sem.at[p], {"patch": q}
        )

    def meta_copy(p, q):
        return remote(
            meta_send.at[q], meta_recv.at[p], msend_sem.at[q], mrecv_sem.at[p], {"patch": q}
        )

    def halo_copy(s, side):
        where = me + 1 if side == 0 else me - 1
        return remote(
            halo_send.at[s, side],
            halo.at[s, side],
            hsend_sem.at[s, side],
            hrecv_sem.at[s, side],
            {"patch": where},
        )

    def vox_copy(side):
        where = me + 1 if side == 0 else me - 1
        return remote(
            vox_send.at[side], vox.at[side], vsend_sem.at[side], vrecv_sem.at[side], {"patch": where}
        )

    has_left, has_right = me > 0, me < n - 1

    def halo_start(s):
        halo_send[s, 0] = ext[s][nblk]
        halo_send[s, 1] = ext[s][1]

        @pl.when(has_right)
        def _():
            halo_copy(s, 0).start()

        @pl.when(has_left)
        def _():
            halo_copy(s, 1).start()

    def halo_take(s):
        @pl.when(has_left)
        def _():
            halo_copy(s, 0).wait_recv()
            ext[s][0] = halo[s, 0]

        @pl.when(has_right)
        def _():
            halo_copy(s, 1).wait_recv()
            ext[s][nblk + 1] = halo[s, 1]

    sub = lax.broadcasted_iota(i32, (128, 128), 0)
    lane = lax.broadcasted_iota(i32, (128, 128), 1)
    eye = sub == lane
    lanes = lane.astype(f32)

    target_row = target_ref[...].astype(f32)
    target_col = jnp.sum(jnp.where(eye, target_row, 0.0), axis=1, keepdims=True)
    same = target_col == target_row
    rank_row = jnp.sum(jnp.where(same & (sub < lane), 1.0, 0.0), axis=0, keepdims=True)
    rank_col = jnp.sum(jnp.where(same & (lane < sub), 1.0, 0.0), axis=1, keepdims=True)
    key_row = ((delay_ref[...] - STEPS) * nblk + source_ref[...]).astype(f32)
    weight_row = weight_ref[...]
    slot_row = jnp.where(rank_row < 16.0, target_row * 16.0 + rank_row, -1.0)
    sel = sub.astype(f32) == slot_row
    q8 = lax.broadcasted_iota(i32, (n, 128), 0).astype(f32)
    sel_over = (q8 == target_row) & (rank_row == 16.0)

    def pick(mask, row):
        return jnp.sum(jnp.where(mask, row, 0.0), axis=1, keepdims=True)

    key = pick(sel, key_row)
    weight = pick(sel, weight_row)
    key_over = pick(sel_over, key_row)
    weight_over = pick(sel_over, weight_row)

    def turn(lag, _):
        old = hist_ref[lag].astype(f32)
        for b in range(nblk):
            ht[lag, pl.ds(b, 8, stride=nblk), :] = old[:, b * 128 : (b + 1) * 128]
        rows = pl.ds(pl.multiple_of(lag * nblk, nblk), nblk)
        for j in range(8):
            hist2[rows, j * 128 : (j + 1) * 128] = ht[lag, j * nblk : (j + 1) * nblk, :].astype(bf16)
        return 0

    def tiles_start(m):
        for side in range(2):
            tile_far(grp, m, side).start()

    def tracts_start(s):
        for d in range(1, n):
            main_copy(s, me, lax.rem(me + d, n)).start()

    pl.semaphore_wait(barrier, n + 1)
    for m in range(STAGES):
        tiles_start(m)
    tile_near(grp).start()

    choose = jnp.where(lanes == key, 1.0, 0.0).astype(bf16)

    def gathered(s):
        low = (STEPS - 1 - s) * nblk
        rows = jnp.dot(choose, hist2[low : low + 128, :], preferred_element_type=f32)
        send[s] = (rows * weight).astype(bf16)

    own_history.wait()
    lax.fori_loop(STEPS - 1, HIST, turn, 0)
    gathered(0)
    tracts_start(0)

    a = jnp.where(q8 == target_row, block_ref[...].astype(f32), 0.0).astype(bf16)
    mef = me.astype(f32)
    b1 = jnp.where((rank_col < 16.0) & (lanes == rank_col + mef * 16.0), 1.0, 0.0).astype(bf16)
    b2 = jnp.where((rank_col == 16.0) & (lanes == mef), 1.0, 0.0).astype(bf16)
    m1 = jnp.dot(a, b1, preferred_element_type=f32)
    m2 = jnp.dot(a, b2, preferred_element_type=f32)
    m = jnp.concatenate([m1, m2], axis=1)
    for q in range(n):
        meta_send[q] = jnp.broadcast_to(m[q : q + 1], (8, 256))

    own_activity.wait()
    for b in range(nblk):
        ext[0][b + 1] = act_ref[:, b * 128 : (b + 1) * 128]
    for s in range(STEPS):
        ext[s][0] = jnp.zeros((8, 128), f32)
        ext[s][nblk + 1] = jnp.zeros((8, 128), f32)

    halo_start(0)
    for d in range(1, n):
        meta_copy(me, lax.rem(me + d, n)).start()
    lax.fori_loop(0, STEPS - 1, turn, 0)
    gathered(1)
    tracts_start(1)
    choose_over = jnp.where(lanes[0:n] == key_over, 1.0, 0.0).astype(bf16)
    for t in range(STEPS):
        low = (STEPS - 1 - t) * nblk
        rows = jnp.dot(choose_over, hist2[low : low + 128, :], preferred_element_type=f32)
        for j in range(8):
            over_f[pl.ds(t * 8 + j, n, stride=32), :] = (
                rows[:, j * 128 : (j + 1) * 128] * weight_over
            )
    for q in range(n):
        over_send[q] = over_f[q * 32 : (q + 1) * 32, :].astype(bf16)
    for d in range(1, n):
        over_copy(me, lax.rem(me + d, n)).start()
    for s in range(2, STEPS):
        gathered(s)
        tracts_start(s)

    mine16 = pl.ds(pl.multiple_of(me * 16, 16), 16)
    for s in range(STEPS):
        recv[s, mine16, :] = send[s, mine16, :]
    over_recv[me] = over_send[me]
    meta_recv[me] = meta_send[me]

    first = ((me - 1) * 128).astype(f32)
    row_id = lax.broadcasted_iota(i32, (288, 128), 0)
    vox_id = (row_id + jnp.where(row_id >= 96, 32, 0) + jnp.where(row_id >= 192, 32, 0)).astype(f32)
    vox_id = vox_id + first

    def member(b, _):
        owner = owner_ref[pl.ds(b, 1), :].astype(f32)
        owned[b] = jnp.where(vox_id == owner, 1.0, 0.0).astype(bf16)
        return 0

    lax.fori_loop(0, nblk, member, 0)

    eye8 = lax.broadcasted_iota(i32, (8, 8), 0) == lax.broadcasted_iota(i32, (8, 8), 1)
    slope = jnp.sum(jnp.where(eye8, slope_ref[...], 0.0), axis=1, keepdims=True)
    strength = jnp.sum(jnp.where(eye8, strength_ref[...], 0.0), axis=1, keepdims=True)
    slope = jnp.broadcast_to(slope, (8, 128))
    strength = jnp.broadcast_to(strength, (8, 128))

    for d in range(1, n):
        p = lax.rem(me + d, n)
        meta_copy(p, me).wait_recv()
        over_copy(p, me).wait_recv()
    where_row = meta_recv[0]
    for p in range(1, n):
        where_row = where_row + meta_recv[p]
    where_row = where_row[0:1, 0:144]
    onehot = jnp.where(
        lax.broadcasted_iota(i32, (nblk, 144), 0).astype(f32) == where_row, 1.0, 0.0
    ).astype(bf16)
    for p in range(n):
        over_f[p * 32 : (p + 1) * 32, :] = over_recv[p].astype(f32)
    for s in range(STEPS):
        extra = jnp.concatenate(
            [over_f[pl.ds(s * 8 + j, n, stride=32), :] for j in range(8)], axis=1
        )
        recv[s, 128:144, :] = jnp.concatenate([extra, jnp.zeros_like(extra)], axis=0).astype(bf16)

    def couple(s):
        for d in range(1, n):
            main_copy(s, lax.rem(me + d, n), me).wait_recv()
        total = jnp.dot(onehot, recv[s], preferred_element_type=f32)
        for j in range(8):
            coupling[s, j * nblk : (j + 1) * nblk, :] = total[:, j * 128 : (j + 1) * 128]

    def update(s, blocks):
        rates = []
        for b in blocks:
            lhs = jnp.concatenate([ext[s][index_ref[k, b]] for k in range(4)], axis=1).astype(bf16)
            rhs = jnp.concatenate([tiles[k, b] for k in range(4)], axis=0)
            local = jnp.dot(lhs, rhs, preferred_element_type=f32)
            tract = coupling[s, pl.ds(b, 8, stride=nblk), :]
            pre = slope * (local + strength * tract + drive_ref[pl.ds(b, 1), :])
            rate = ext[s][b + 1]
            rates.append(rate + 0.5 * (jax.nn.sigmoid(pre) - rate))
        for b, rate in zip(blocks, rates):
            ext[s + 1][b + 1] = rate

    def region(s, m):
        if s > m:
            return set()
        reach = (m + 1) * wide_part - s
        if m == STAGES - 1:
            reach = nblk // 2
        return set(range(reach)) | set(range(nblk - reach, nblk))

    def step(s, m):
        todo = sorted(region(s, m) - (region(s, m - 1) if m > 0 else set()))
        for i in range(0, len(todo), 16):
            update(s, todo[i : i + 16])

    own_tiles.wait()
    tile_near(near).wait_recv()
    other = lax.rem(near + 2, groups)
    for m in range(STAGES):
        for side in range(2):
            tile_far(grp, m, side).wait_send()
        for d in range(1, n):
            main_copy(m, me, lax.rem(me + d, n)).wait_send()
        for side in range(2):
            tile_far(far, m, side).wait_recv()
            tile_relay(far, m, side).start()
        couple(m)
        for side in range(2):
            tile_relay(other, m, side).wait_recv()
        for s in range(m + 1):
            if s == m:
                halo_take(s)
            step(s, m)
            if s == m and s + 1 < STEPS:
                halo_start(s + 1)

    ones = jnp.ones((64, 512), bf16)

    def sums(i, total):
        rates = [
            jnp.concatenate([ext[s + 1][i * 4 + u + 1] for u in range(4)], axis=1)
            for s in range(STEPS)
        ]
        rates = jnp.concatenate(rates, axis=0)
        high = rates.astype(bf16)
        low = (rates - high.astype(f32)).astype(bf16)
        lhs = jnp.concatenate([high, low, ones], axis=0)
        rhs = jnp.concatenate([owned[i * 4 + u] for u in range(4)], axis=1)
        return total + lax.dot_general(
            rhs, lhs, (((1,), (1,)), ((), ())), preferred_element_type=f32
        )

    total = jnp.zeros((288, 128), f32)
    for i in range(nblk // 4):
        total = sums(i, total)

    def of_patch(i):
        rows = jnp.concatenate([total[i * 96 : (i + 1) * 96], jnp.zeros((32, 128), f32)], axis=0).T
        return jnp.concatenate([rows[0:32] + rows[32:64], rows[64:72]], axis=0)

    vox_send[0] = of_patch(2)
    vox_send[1] = of_patch(0)

    @pl.when(has_right)
    def _():
        vox_copy(0).start()

    @pl.when(has_left)
    def _():
        vox_copy(1).start()

    vox_send[2] = of_patch(1)
    for b in range(nblk):
        act_out[:, b * 128 : (b + 1) * 128] = ext[STEPS][b + 1]

    @pl.when(has_left)
    def _():
        vox_copy(0).wait_recv()
        vox_send[2] = vox_send[2] + vox[0]

    @pl.when(has_right)
    def _():
        vox_copy(1).wait_recv()
        vox_send[2] = vox_send[2] + vox[1]

    floor = jnp.maximum(vox_send[2, 32:40, :], 1.0)
    vaso = vaso_ref[...]
    flow = flow_ref[...]
    for s in range(STEPS):
        level = vox_send[2, s * 8 : s * 8 + 8, :] / floor
        vaso = vaso + 0.5 * (level - 0.65 * vaso - 0.41 * (flow - 1.0))
        flow = flow + 0.5 * vaso
    vaso_out[...] = vaso
    flow_out[...] = flow

    for d in range(1, n):
        q = lax.rem(me + d, n)
        over_copy(me, q).wait_send()
        meta_copy(me, q).wait_send()
    tile_near(grp).wait_send()
    for m in range(STAGES):
        for side in range(2):
            tile_relay(far, m, side).wait_send()

    @pl.when(has_right)
    def _():
        for s in range(STEPS):
            halo_copy(s, 0).wait_send()
        vox_copy(0).wait_send()

    @pl.when(has_left)
    def _():
        for s in range(STEPS):
            halo_copy(s, 1).wait_send()
        vox_copy(1).wait_send()


def hand_on(a, b, c, a_out, b_out, c_out):
    a_out[...] = a[...]
    b_out[...] = b[...]
    c_out[...] = c[...]


def fused(
    activity,
    history,
    drive,
    slope,
    strength,
    kernel,
    kernel_index,
    tract_source,
    tract_delay,
    tract_target,
    tract_block,
    tract_weight,
    voxel_owner,
    vaso_signal,
    blood_flow,
):
    n, groups = lax.axis_size("patch"), lax.axis_size("trial")
    f32, bf16 = jnp.float32, jnp.bfloat16
    vmem = pl.BlockSpec(memory_space=pltpu.VMEM)
    smem = pl.BlockSpec(memory_space=pltpu.SMEM)
    dma = pltpu.SemaphoreType.DMA
    hbm = pl.BlockSpec(memory_space=pltpu.HBM)
    scratch = [
        pltpu.VMEM(activity.shape, f32),
        pltpu.VMEM(history.shape, bf16),
        pltpu.VMEM((HIST, 256, 128), f32),
        pltpu.VMEM((HIST * 32, 1024), bf16),
        pltpu.VMEM((STEPS, 128, 1024), bf16),
        pltpu.VMEM((STEPS, 144, 1024), bf16),
        pltpu.VMEM((256, 128), f32),
        pltpu.VMEM((n, 32, 128), bf16),
        pltpu.VMEM((n, 32, 128), bf16),
        pltpu.VMEM((n, 8, 256), f32),
        pltpu.VMEM((n, 8, 256), f32),
        pltpu.VMEM((4, 32, 128, 128), bf16),
        *[pltpu.VMEM((34, 8, 128), f32) for _ in range(STEPS + 1)],
        pltpu.VMEM((STEPS, 2, 8, 128), f32),
        pltpu.VMEM((STEPS, 2, 8, 128), f32),
        pltpu.VMEM((STEPS, 256, 128), f32),
        pltpu.VMEM((32, 288, 128), bf16),
        pltpu.VMEM((3, 40, 128), f32),
        pltpu.VMEM((2, 40, 128), f32),
        dma((STEPS, n)),
        dma((STEPS, n)),
        dma((n,)),
        dma((n,)),
        dma((n,)),
        dma((n,)),
        dma((STAGES, 2)),
        dma((STAGES, 2)),
        dma((STAGES, 2)),
        dma((STAGES, 2)),
        dma((2,)),
        dma((STEPS, 2)),
        dma((STEPS, 2)),
        dma((2,)),
        dma((2,)),
        dma((3,)),
    ]
    results = pl.pallas_call(
        functools.partial(window, n, groups),
        out_shape=(
            jax.ShapeDtypeStruct(activity.shape, f32),
            jax.ShapeDtypeStruct(vaso_signal.shape, f32),
            jax.ShapeDtypeStruct(blood_flow.shape, f32),
        ),
        in_specs=[hbm] * 2 + [vmem] * 3 + [hbm, smem] + [vmem] * 8,
        out_specs=(vmem, vmem, vmem),
        scratch_shapes=scratch,
        compiler_params=pltpu.CompilerParams(
            collective_id=0, has_side_effects=True, vmem_limit_bytes=62 * 1024 * 1024
        ),
    )(
        activity,
        history,
        drive.reshape(32, 128),
        slope.reshape(1, 8),
        strength.reshape(1, 8),
        kernel.reshape(32, 128, 128),
        kernel_index.T,
        tract_source.reshape(1, 128),
        tract_delay.reshape(1, 128),
        tract_target.reshape(1, 128),
        tract_block.reshape(1, 128),
        tract_weight.reshape(1, 128),
        voxel_owner.reshape(32, 128),
        vaso_signal,
        blood_flow,
    )
    return pl.pallas_call(
        hand_on,
        out_shape=tuple(jax.ShapeDtypeStruct(r.shape, r.dtype) for r in results),
        in_specs=[vmem] * 3,
        out_specs=(vmem, vmem, vmem),
        compiler_params=pltpu.CompilerParams(vmem_limit_bytes=62 * 1024 * 1024),
    )(*results)


def planned(*args):
    shapes = (
        lax.axis_size("patch"),
        lax.axis_size("trial"),
        args[0].shape,
        args[7].shape,
        args[13].shape,
    )
    if shapes == (8, 4, (8, 4096), (128,), (8, 128)):
        return fused(*args)
    return shards(*args)


def solution(mesh):
    placed = (
        P("trial", "patch"),
        P(None, "trial", "patch"),
        P("patch"),
        P("trial"),
        P("trial"),
        P("patch", "trial", None, None),
        P("patch", None),
        P("patch"),
        P("patch"),
        P("patch", None),
        P("patch"),
        P("patch"),
        P("patch"),
        P("trial", "patch"),
        P("trial", "patch"),
    )
    return jax.shard_map(
        planned,
        mesh=mesh,
        in_specs=placed,
        out_specs=(P("trial", "patch"), P("trial", "patch"), P("trial", "patch")),
        check_vma=False,
    )
```
